512 devices in a mesh: dp: 512 (over y, z, x, core).
Axes of the slice: x: 4, y: 8, z: 8, core: 2. Of those that a mesh axis runs over, the one named last changes fastest.
Arguments:
- video_emb: bfloat16 [196608, 640], P('dp'), may hold values from -6 to 6
- captions: bfloat16 [196608, 1152], P('dp'), may hold values from -0.29882812 to 0.29882812
- projection: bfloat16 [1152, 640], replicated, may hold values from -0.0068359375 to 0.0068359375
- labels: int32 [196608], P('dp'), may hold values 0 or 1
- log_scale: float32 [1], replicated, may hold values from 1.5 to 2.5
- bias: float32 [1], replicated, may hold values from -3 to -1
Outputs:
- caption_grad: bfloat16 [196608, 1152], P('dp')
- projection_grad: bfloat16 [1152, 640], replicated
The draws below stay inside these ranges and needn't reach their ends.
All inputs are finite; a program needn't handle non-finite values. No bound on the sum of `labels` on one device may be relied on, other than what follows from the above.
Results may differ from the reference program's by a relative error of at most 0.014.
Values may be sent and summed in bfloat16 or wider, within the bound.
A program may use at most 64 MiB of HBM per device.

```python
import jax
import jax.numpy as jnp
import numpy as np
from jax import lax

D = 1152
E = 640
B = 384
ROUNDS = 4
BLOCKS = 512
TOKENS = 196608
N_DP = 512


def with_ends(entries, key, least, high):
    spot = [jax.random.randint(jax.random.fold_in(key, axis), (), 0, length) for axis, length in enumerate(entries.shape)]
    main_axis = entries.shape.index(max(entries.shape))
    beside = spot[:main_axis] + [(spot[main_axis] + 1) % entries.shape[main_axis]] + spot[main_axis + 1:]
    return entries.at[tuple(spot)].set(least).at[tuple(beside)].set(high)


def steps_of(own_key, shape, split, smallest, high):
    def one(dim, shards_of):
        steps = jax.random.uniform(jax.random.fold_in(jax.random.fold_in(own_key, 6), dim), (shards_of,), jnp.float32, smallest / len(split), high / len(split))
        return jnp.repeat(jnp.exp(steps), shape[dim] // shards_of).reshape((-1,) + (1,) * (len(shape) - dim - 1))

    loudness = one(*split[0])
    for cut in split[1:]:
        loudness = loudness * one(*cut)
    return loudness


def bell_draw(stream_key, shape, scale, most, pieces=(), kind=jnp.bfloat16):
    values = jax.random.normal(stream_key, shape, jnp.float32) * scale
    if len(pieces) > 0:
        values = steps_of(stream_key, shape, pieces, -0.22, 0.18) * values
    return jnp.clip(values, min=-most, max=most).astype(kind)


def setup_inputs(seed: int = 0) -> dict:
    streams_of = jax.random.split(jax.random.key(seed), 7)
    video_emb = bell_draw(streams_of[0], (TOKENS, E), 1.0, 6.0, ((0, 512),))
    captions = bell_draw(streams_of[1], (TOKENS, D), 0.05, 0.29882812, ((0, 512),))
    projection = bell_draw(streams_of[2], (D, E), (D * E) ** -0.5, 0.0068359375)
    labels = with_ends((jax.random.randint(streams_of[3], (TOKENS,), 0, 4) < 3).astype(jnp.int32), jax.random.fold_in(streams_of[3], 1), 0, 1)
    log_scale = jnp.clip(jax.random.uniform(streams_of[4], (1,), jnp.float32, 1.5, 2.5), 1.5, 2.5)
    bias = jnp.clip(jax.random.uniform(streams_of[5], (1,), jnp.float32, -3.0, -1.0), -3.0, -1.0)
    return {"video_emb": video_emb, "captions": captions, "projection": projection, "labels": labels, "log_scale": log_scale, "bias": bias}


def unit_rows(values):
    inverse = lax.rsqrt(lax.optimization_barrier(jnp.sum(values * values, axis=-1, keepdims=True)) + 1e-06)
    return (values * inverse, inverse)

def reference(video_emb, captions, projection, labels, log_scale, bias):
    count = BLOCKS
    rows = B
    scale = jnp.exp(log_scale[0])
    shift = bias[0]
    zv_round = lax.optimization_barrier(unit_rows(video_emb.astype(jnp.float32))[0].astype(jnp.bfloat16))
    zv = zv_round.astype(jnp.float32).reshape(count, rows, E)
    hidden = jnp.dot(captions, projection, preferred_element_type=jnp.float32)
    zf, inverse = unit_rows(hidden)
    zc_round = lax.optimization_barrier(zf.astype(jnp.bfloat16))
    zc = zc_round.astype(jnp.float32).reshape(count, rows, E)
    level = N_DP.bit_length() - 1
    positive = (labels.reshape(count, rows) == 1)[:, None, :] & jnp.eye(rows, dtype=bool)[None, :, :]
    own_sign = jnp.where(positive, 1.0, -1.0).astype(jnp.float32)
    pairings = [np.arange(count)]
    for step in range(ROUNDS):
        pairings.append(np.arange(count) ^ 1 << step * (level - 1) // 3)
    dz = jnp.zeros((count, rows, E), jnp.float32)
    for index, partner in enumerate(pairings):
        zvp = zv[partner]
        logits = scale * jnp.einsum('nae,nbe->nab', zvp, zc, precision=lax.Precision.HIGHEST) + shift
        if index == 0:
            weight = -own_sign * jax.nn.sigmoid(-own_sign * logits)
        else:
            weight = jax.nn.sigmoid(logits)
        weight = lax.optimization_barrier(weight.astype(jnp.bfloat16)).astype(jnp.float32)
        dz = dz + scale * jnp.einsum('nab,nae->nbe', weight, zvp, precision=lax.Precision.HIGHEST)
    dz = dz.reshape(count * rows, E)
    dh = (inverse * (dz - zf * lax.optimization_barrier(jnp.sum(zf * dz, axis=-1, keepdims=True)))).astype(jnp.bfloat16)
    caption_grad = jnp.dot(dh, projection.T, preferred_element_type=jnp.float32).astype(jnp.bfloat16)
    projection_grad = (jnp.dot(captions.T, dh, preferred_element_type=jnp.float32) / count).astype(jnp.bfloat16)
    return (caption_grad, projection_grad)
```

```python
import functools

import jax
import jax.numpy as jnp
from jax import lax
from jax.experimental import pallas as pl
from jax.experimental.pallas import tpu as pltpu
from jax.sharding import PartitionSpec as P

MESH = pl.DeviceIdType.MESH
F32 = jnp.float32
BF16 = jnp.bfloat16

AXES = {"core": (1, 2), "x": (2, 4), "z": (8, 8), "y": (64, 8)}
SIZE = {axis: size for axis, (_, size) in AXES.items()}

ROWS = 384
E = 640
D = 1152
HALF = D // 2
CHUNKS = 3
CHUNK = ROWS // (2 * CHUNKS)
LANES = 128
COLS = E // LANES

ORDERS = (("x", "y", "z"), ("y", "z", "x"), ("z", "x", "y"))
PARTS = len(ORDERS)
PART = HALF // PARTS
FLAT = PART * COLS
FULL = 1024


def place(me, axis):
    stride, size = AXES[axis]
    return lax.rem(lax.div(me, stride), size)


def shifted(me, axis, by):
    stride, size = AXES[axis]
    here = place(me, axis)
    return me + (lax.rem(here + (by + size), size) - here) * stride


def remote(src, dst, send, recv, device):
    return pltpu.make_async_remote_copy(
        src_ref=src, dst_ref=dst, send_sem=send, recv_sem=recv, device_id=(device,), device_id_type=MESH
    )


def far_first(size):
    return sorted(range(1, size), key=lambda by: -min(by, size - by))


def kernel(
    video_ref, captions_ref, projection_ref, labels_ref, log_scale_ref, bias_ref,
    cgrad_ref, pgrad_ref,
    video, captions, projection, flipped, zf, zc, inv, dz, dh, cgrad,
    own_core, own_x, relay_x, pool, relay,
    out_core, in_core, own_term,
    s1_out, s1_in, s2_out, s2_in, s3_in, gather2, gather1,
    load_sem, swap_send, swap_recv, hop_send, hop_recv, core_send, core_recv,
    stage_send, stage_recv, last_sem, last_send, last_recv,
):
    me = lax.axis_index("dp")
    core = place(me, "core")
    sibling = shifted(me, "core", 1)

    loads = [
        pltpu.make_async_copy(video_ref, video, load_sem.at[0]),
        pltpu.make_async_copy(captions_ref, captions, load_sem.at[1]),
        pltpu.make_async_copy(projection_ref, projection, load_sem.at[2]),
    ]
    for load in loads:
        load.start()

    barrier = pltpu.get_barrier_semaphore()
    greeted = 0
    for axis, size in SIZE.items():
        for by in range(1, size):
            pl.semaphore_signal(barrier, inc=1, device_id=(shifted(me, axis, by),), device_id_type=MESH)
            greeted += 1
    pl.semaphore_wait(barrier, greeted)
    loads[0].wait()

    ways = [("y", 1, 2), ("y", -1, 2), ("z", 1, 2), ("z", -1, 2), ("x", 1, 1), ("x", -1, 1)]
    hops = []
    for q in range(CHUNKS):
        for w, (axis, way, step) in enumerate(ways):
            rows = pl.ds(((0 if way > 0 else CHUNKS) + q) * CHUNK, CHUNK)
            if axis == "x":
                middle, final = relay_x.at[rows], own_x.at[rows]
            else:
                middle, final = relay.at[w, q], pool.at[q, pl.ds(w * CHUNK, CHUNK)]
            to = shifted(me, axis, way * step)
            first = remote(video.at[rows], middle, hop_send.at[w, q, 0], hop_recv.at[w, q, 0], to)
            second = remote(middle, final, hop_send.at[w, q, 1], hop_recv.at[w, q, 1], to)
            first.start()
            hops.append((first, second))
        if q == 0:
            swap = remote(video, own_core, swap_send, swap_recv, sibling)
            swap.start()

    def pass_on(q):
        for first, second in hops[q * len(ways):(q + 1) * len(ways)]:
            first.wait_recv()
            second.start()

    scale = jnp.exp(jnp.full((1, 1), log_scale_ref[0], F32))
    shift = bias_ref[0]

    loads[1].wait()
    loads[2].wait()
    hidden = jnp.dot(captions[...], projection[...], preferred_element_type=F32)
    inverse = lax.rsqrt(jnp.sum(hidden * hidden, axis=-1, keepdims=True) + 1e-06)
    unit = hidden * inverse
    zf[...] = unit
    zc[...] = unit.astype(BF16)
    inv[...] = inverse

    def pairing(rows, sign=None):
        raw = rows.astype(F32)
        zv = (raw * lax.rsqrt(jnp.sum(raw * raw, axis=-1, keepdims=True) + 1e-06)).astype(BF16)
        logits = scale * lax.dot_general(
            zc[...], zv, (((1,), (1,)), ((), ())), preferred_element_type=F32
        ) + shift
        if sign is None:
            weight = 1.0 / (1.0 + jnp.exp(-logits))
        else:
            weight = sign / (1.0 + jnp.exp(-sign * logits))
        return jnp.dot(weight.astype(BF16), zv, preferred_element_type=F32)

    pass_on(0)
    row = lax.broadcasted_iota(jnp.int32, (ROWS, ROWS), 0)
    column = lax.broadcasted_iota(jnp.int32, (ROWS, ROWS), 1)
    sign = jnp.where((row == column) & (labels_ref[...] == 1), -1.0, 1.0).astype(F32)
    dz[...] = pairing(video[...], sign)
    pass_on(1)
    swap.wait_recv()
    dz[...] += pairing(own_core[...])
    pass_on(2)
    flipped[...] = captions[...].T
    for q in range(CHUNKS):
        for first, second in hops[q * len(ways) + 4:(q + 1) * len(ways)]:
            second.wait_recv()
    dz[...] += pairing(own_x[...])
    for q in range(CHUNKS):
        for first, second in hops[q * len(ways):q * len(ways) + 4]:
            second.wait_recv()
        dz[...] += pairing(pool[q])

    total = scale * dz[...]
    along = jnp.sum(zf[...] * total, axis=-1, keepdims=True)
    dh[...] = (inv[...] * (total - zf[...] * along)).astype(BF16)

    def term(half, part):
        rows = pl.ds(pl.multiple_of(half * HALF + part * PART, 16), PART)
        return jnp.dot(flipped[rows, :], dh[...], preferred_element_type=F32)

    to_core = []
    for p in range(PARTS):
        value = term(1 - core, p).astype(BF16)
        for j in range(COLS):
            out_core[p, j * PART:(j + 1) * PART, :] = value[:, j * LANES:(j + 1) * LANES]
        copy = remote(out_core.at[p], in_core.at[p], core_send.at[p], core_recv.at[p], sibling)
        copy.start()
        to_core.append(copy)
    for p in range(PARTS):
        value = term(core, p)
        for j in range(COLS):
            own_term[p, j * PART:(j + 1) * PART, :] = value[:, j * LANES:(j + 1) * LANES]

    pending = list(to_core)

    def start_all(stage, p, axis, src_of, dst_of):
        copies = []
        for by in far_first(SIZE[axis]):
            copy = remote(
                src_of(by), dst_of(by), stage_send.at[stage, p, by], stage_recv.at[stage, p, by], shifted(me, axis, by)
            )
            copy.start()
            copies.append(copy)
        pending.extend(copies)
        return copies

    arrivals = [None] * PARTS
    for p, (axis, _, _) in enumerate(ORDERS):
        to_core[p].wait_recv()
        s1_out[p, :FLAT, :] = (own_term[p] + in_core[p].astype(F32)).astype(BF16)
        s1_out[p, FLAT:, :] = jnp.zeros((FULL - FLAT, LANES), BF16)
        n = SIZE[axis]
        rows = FULL // n
        here = place(me, axis)
        arrivals[p] = start_all(
            0, p, axis,
            lambda by: s1_out.at[p, pl.ds(pl.multiple_of(lax.rem(here + by, n) * rows, 16), rows)],
            lambda by: s1_in.at[p, by, pl.ds(0, rows)],
        )

    cgrad[...] = lax.dot_general(
        dh[...], projection[...], (((1,), (1,)), ((), ())), preferred_element_type=F32
    ).astype(BF16)
    store = pltpu.make_async_copy(cgrad, cgrad_ref, last_sem.at[0])
    store.start()

    for p, (axis1, axis2, _) in enumerate(ORDERS):
        for copy in arrivals[p]:
            copy.wait_recv()
        n1, n2 = SIZE[axis1], SIZE[axis2]
        rows1 = FULL // n1
        rows2 = rows1 // n2
        mine = pl.ds(pl.multiple_of(place(me, axis1) * rows1, 16), rows1)
        value = s1_out[p, mine, :].astype(F32)
        for by in range(1, n1):
            value += s1_in[p, by, :rows1, :].astype(F32)
        s2_out[p, :rows1, :] = value.astype(BF16)
        here = place(me, axis2)
        arrivals[p] = start_all(
            1, p, axis2,
            lambda by: s2_out.at[p, pl.ds(pl.multiple_of(lax.rem(here + by, n2) * rows2, 16), rows2)],
            lambda by: s2_in.at[p, by, pl.ds(0, rows2)],
        )

    for p, (axis1, axis2, axis3) in enumerate(ORDERS):
        for copy in arrivals[p]:
            copy.wait_recv()
        n2 = SIZE[axis2]
        rows2 = FULL // SIZE[axis1] // n2
        mine = pl.ds(pl.multiple_of(place(me, axis2) * rows2, 16), rows2)
        value = s2_out[p, mine, :].astype(F32)
        for by in range(1, n2):
            value += s2_in[p, by, :rows2, :].astype(F32)
        here = place(me, axis3)
        s3_in[p, here, :rows2, :] = value.astype(BF16)
        slot = s3_in.at[p, here, pl.ds(0, rows2)]
        arrivals[p] = start_all(2, p, axis3, lambda by: slot, lambda by: slot)

    devices = 1
    for size in SIZE.values():
        devices *= size

    for p, (axis1, axis2, axis3) in enumerate(ORDERS):
        for copy in arrivals[p]:
            copy.wait_recv()
        rows2 = FULL // SIZE[axis1] // SIZE[axis2]
        value = s3_in[p, 0, :rows2, :].astype(F32)
        for k in range(1, SIZE[axis3]):
            value += s3_in[p, k, :rows2, :].astype(F32)
        mine = pl.ds(pl.multiple_of(place(me, axis2) * rows2, 16), rows2)
        gather2[p, mine, :] = (value / devices).astype(BF16)
        slot = gather2.at[p, mine]
        arrivals[p] = start_all(3, p, axis2, lambda by: slot, lambda by: slot)

    for p, (axis1, _, _) in enumerate(ORDERS):
        for copy in arrivals[p]:
            copy.wait_recv()
        rows1 = FULL // SIZE[axis1]
        mine = pl.ds(pl.multiple_of(place(me, axis1) * rows1, 16), rows1)
        gather1[p, mine, :] = gather2[p, :rows1, :]
        slot = gather1.at[p, mine]
        arrivals[p] = start_all(4, p, axis1, lambda by: slot, lambda by: slot)

    writes = []
    for p in range(PARTS):
        for copy in arrivals[p]:
            copy.wait_recv()
        for j in range(COLS):
            src = gather1.at[p, pl.ds(j * PART, PART)]
            dst = pgrad_ref.at[
                pl.ds(pl.multiple_of(core * HALF + p * PART, 16), PART), pl.ds(j * LANES, LANES)
            ]
            copy = remote(src, dst, last_send.at[p, j], last_recv.at[p, j], sibling)
            copy.start()
            write = pltpu.make_async_copy(src, dst, last_sem.at[1 + p * COLS + j])
            write.start()
            writes.append((copy, write))
    for copy, write in writes:
        copy.wait()
        write.wait()

    store.wait()
    swap.wait_send()
    for first, second in hops:
        first.wait_send()
        second.wait_send()
    for copy in pending:
        copy.wait_send()


def local(video_emb, captions, projection, labels, log_scale, bias):
    dma = pltpu.SemaphoreType.DMA
    vmem = pltpu.VMEM
    shard = FULL // 4
    return pl.pallas_call(
        kernel,
        out_shape=(
            jax.ShapeDtypeStruct((ROWS, D), BF16),
            jax.ShapeDtypeStruct((D, E), BF16),
        ),
        in_specs=[pl.BlockSpec(memory_space=pl.ANY)] * 3
        + [pl.BlockSpec(memory_space=pltpu.VMEM)]
        + [pl.BlockSpec(memory_space=pltpu.SMEM)] * 2,
        out_specs=[pl.BlockSpec(memory_space=pl.ANY)] * 2,
        scratch_shapes=[
            vmem((ROWS, E), BF16),
            vmem((ROWS, D), BF16),
            vmem((D, E), BF16),
            vmem((D, ROWS), BF16),
            vmem((ROWS, E), F32),
            vmem((ROWS, E), BF16),
            vmem((ROWS, 1), F32),
            vmem((ROWS, E), F32),
            vmem((ROWS, E), BF16),
            vmem((ROWS, D), BF16),
            vmem((ROWS, E), BF16),
            vmem((ROWS, E), BF16),
            vmem((ROWS, E), BF16),
            vmem((CHUNKS, 4 * CHUNK, E), BF16),
            vmem((4, CHUNKS, CHUNK, E), BF16),
            vmem((PARTS, FLAT, LANES), BF16),
            vmem((PARTS, FLAT, LANES), BF16),
            vmem((PARTS, FLAT, LANES), F32),
            vmem((PARTS, FULL, LANES), BF16),
            vmem((PARTS, 8, shard, LANES), BF16),
            vmem((PARTS, shard, LANES), BF16),
            vmem((PARTS, 8, 32, LANES), BF16),
            vmem((PARTS, 8, 32, LANES), BF16),
            vmem((PARTS, shard, LANES), BF16),
            vmem((PARTS, FULL, LANES), BF16),
            dma((3,)),
            dma,
            dma,
            dma((6, CHUNKS, 2)),
            dma((6, CHUNKS, 2)),
            dma((PARTS,)),
            dma((PARTS,)),
            dma((5, PARTS, 8)),
            dma((5, PARTS, 8)),
            dma((1 + PARTS * COLS,)),
            dma((PARTS, COLS)),
            dma((PARTS, COLS)),
        ],
        compiler_params=pltpu.CompilerParams(
            collective_id=0, has_side_effects=True, vmem_limit_bytes=48 << 20
        ),
    )(video_emb, captions, projection, labels.reshape(1, -1), log_scale, bias)


def solution(mesh):
    return jax.shard_map(
        local,
        mesh=mesh,
        in_specs=(P("dp", None), P("dp", None), P(), P("dp"), P(), P()),
        out_specs=(P("dp", None), P()),
        check_vma=False,
    )
```

```python
import functools

import jax
import jax.numpy as jnp
from jax import lax
from jax.experimental import pallas as pl
from jax.experimental.pallas import tpu as pltpu
from jax.sharding import PartitionSpec as P

MESH = pl.DeviceIdType.MESH
F32 = jnp.float32
BF16 = jnp.bfloat16

AXES = {"core": (1, 2), "x": (2, 4), "z": (8, 8), "y": (64, 8)}
SIZE = {axis: size for axis, (_, size) in AXES.items()}

ROWS = 384
E = 640
D = 1152
HALF = D // 2
CHUNKS = 3
CHUNK = ROWS // CHUNKS
LANES = 128
COLS = E // LANES
TILE = 16

ORDERS = (("y", "z", "x"), ("z", "x", "y"), ("x", "y", "z"))
PART = (144, 144, 288)
FIRST = (0, 144, 288)
PARTS = len(ORDERS)


def up(value, multiple):
    return -(-value // multiple) * multiple


FLAT = tuple(rows * COLS for rows in PART)
SUM1 = tuple(up(-(-FLAT[p] // SIZE[ORDERS[p][0]]), TILE) for p in range(PARTS))
SUM2 = tuple(up(-(-SUM1[p] // SIZE[ORDERS[p][1]]), TILE) for p in range(PARTS))
FULL1 = tuple(SUM1[p] * SIZE[ORDERS[p][0]] for p in range(PARTS))
FULL2 = tuple(SUM2[p] * SIZE[ORDERS[p][1]] for p in range(PARTS))


def place(me, axis):
    stride, size = AXES[axis]
    return lax.rem(lax.div(me, stride), size)


def shifted(me, axis, by):
    stride, size = AXES[axis]
    here = place(me, axis)
    return me + (lax.rem(here + (by + size), size) - here) * stride


def remote(src, dst, send, recv, device):
    return pltpu.make_async_remote_copy(
        src_ref=src, dst_ref=dst, send_sem=send, recv_sem=recv, device_id=(device,), device_id_type=MESH
    )


def far_first(size):
    return sorted(range(1, size), key=lambda by: -min(by, size - by))


def kernel(
    video_ref, captions_ref, projection_ref, labels_ref, log_scale_ref, bias_ref,
    cgrad_ref, pgrad_ref,
    video, captions, projection, flipped, zf, zc, inv, dz, dh, cgrad,
    own_core, own_x, pool,
    out_core, in_core, own_term, s1_out, s1_in, s2_out, s2_in, s3_in, gather2, gather1, result,
    load_sem, swap_send, swap_recv, core_send, core_recv,
    stage_send, stage_recv, last_sem, last_send, last_recv, round_sem,
):
    me = lax.axis_index("dp")
    core = place(me, "core")
    sibling = shifted(me, "core", 1)

    loads = [
        pltpu.make_async_copy(video_ref, video, load_sem.at[0]),
        pltpu.make_async_copy(captions_ref, captions, load_sem.at[1]),
        pltpu.make_async_copy(projection_ref, projection, load_sem.at[2]),
    ]
    for load in loads:
        load.start()

    barrier = pltpu.get_barrier_semaphore()
    greeted = [(axis, SIZE[axis] // 2) for axis in ("y", "z", "x")]
    greeted += [(axis, by) for axis in ("y", "z", "x") for by in (1, -1)] + [("core", 1)]
    for axis, by in greeted:
        pl.semaphore_signal(barrier, inc=1, device_id=(shifted(me, axis, by),), device_id_type=MESH)
    pl.semaphore_wait(barrier, len(greeted))
    loads[0].wait()

    swaps = []
    for q in range(CHUNKS):
        rows = pl.ds(q * CHUNK, CHUNK)
        for w, axis in enumerate(("y", "z")):
            swap = remote(
                video.at[rows], pool.at[q, pl.ds(w * CHUNK, CHUNK)], swap_send.at[w, q], swap_recv.at[w, q],
                shifted(me, axis, SIZE[axis] // 2),
            )
            swap.start()
            swaps.append(swap)
        if q == 0:
            swap_x = remote(video, own_x, swap_send.at[2, 0], swap_recv.at[2, 0], shifted(me, "x", SIZE["x"] // 2))
            swap_x.start()
            swap_core = remote(video, own_core, swap_send.at[3, 0], swap_recv.at[3, 0], sibling)
            swap_core.start()

    neighbours = [("y", 1), ("y", -1), ("z", 1), ("z", -1)]
    for axis, by in neighbours:
        pl.semaphore_signal(round_sem, inc=1, device_id=(shifted(me, axis, by),), device_id_type=MESH)

    scale = jnp.exp(jnp.full((1, 1), log_scale_ref[0], F32))
    shift = bias_ref[0]

    loads[1].wait()
    loads[2].wait()
    hidden = jnp.dot(captions[...], projection[...], preferred_element_type=F32)
    inverse = lax.rsqrt(jnp.sum(hidden * hidden, axis=-1, keepdims=True) + 1e-06)
    unit = hidden * inverse
    zf[...] = unit
    zc[...] = unit.astype(BF16)
    inv[...] = inverse

    def pairing(rows, sign=None):
        raw = rows.astype(F32)
        zv = (raw * lax.rsqrt(jnp.sum(raw * raw, axis=-1, keepdims=True) + 1e-06)).astype(BF16)
        logits = scale * lax.dot_general(
            zc[...], zv, (((1,), (1,)), ((), ())), preferred_element_type=F32
        ) + shift
        if sign is None:
            weight = 1.0 / (1.0 + jnp.exp(-logits))
        else:
            weight = sign / (1.0 + jnp.exp(-sign * logits))
        return jnp.dot(weight.astype(BF16), zv, preferred_element_type=F32)

    row = lax.broadcasted_iota(jnp.int32, (ROWS, ROWS), 0)
    column = lax.broadcasted_iota(jnp.int32, (ROWS, ROWS), 1)
    sign = jnp.where((row == column) & (labels_ref[...].reshape(1, ROWS) == 1), -1.0, 1.0).astype(F32)
    dz[...] = pairing(video[...], sign)
    flipped[...] = captions[...].T
    pl.semaphore_wait(round_sem, len(neighbours))
    swap_core.wait_recv()
    dz[...] += pairing(own_core[...])
    swap_x.wait_recv()
    dz[...] += pairing(own_x[...])
    for q in range(CHUNKS):
        for swap in swaps[2 * q:2 * q + 2]:
            swap.wait_recv()
        dz[...] += pairing(pool[q])

    total = scale * dz[...]
    along = jnp.sum(zf[...] * total, axis=-1, keepdims=True)
    dh[...] = (inv[...] * (total - zf[...] * along)).astype(BF16)

    def term(half, part):
        rows = pl.ds(pl.multiple_of(half * HALF + FIRST[part], TILE), PART[part])
        return jnp.dot(flipped[rows, :], dh[...], preferred_element_type=F32)

    to_core = []
    for p in range(PARTS):
        value = term(1 - core, p).astype(BF16)
        for j in range(COLS):
            out_core[p][j * PART[p]:(j + 1) * PART[p], :] = value[:, j * LANES:(j + 1) * LANES]
        copy = remote(out_core[p], in_core[p], core_send.at[p], core_recv.at[p], sibling)
        copy.start()
        to_core.append(copy)
    for p in range(PARTS):
        value = term(core, p)
        for j in range(COLS):
            own_term[p][j * PART[p]:(j + 1) * PART[p], :] = value[:, j * LANES:(j + 1) * LANES]

    pending = list(to_core)

    def start_all(stage, p, axis, src_of, dst_of):
        copies = []
        for by in far_first(SIZE[axis]):
            copy = remote(
                src_of(by), dst_of(by), stage_send.at[stage, p, by], stage_recv.at[stage, p, by], shifted(me, axis, by)
            )
            copy.start()
            copies.append(copy)
        pending.extend(copies)
        return copies

    def slot(axis, rows):
        return pl.ds(pl.multiple_of(place(me, axis) * rows, TILE), rows)

    def slot_of(axis, by, rows):
        return pl.ds(pl.multiple_of(lax.rem(place(me, axis) + by, SIZE[axis]) * rows, TILE), rows)

    arrivals = [None] * PARTS
    for p, (axis, _, _) in enumerate(ORDERS):
        to_core[p].wait_recv()
        s1_out[p][:FLAT[p], :] = (own_term[p][...] + in_core[p][...].astype(F32)).astype(BF16)
        if FULL1[p] > FLAT[p]:
            s1_out[p][FLAT[p]:, :] = jnp.zeros((FULL1[p] - FLAT[p], LANES), BF16)
        arrivals[p] = start_all(
            0, p, axis, lambda by: s1_out[p].at[slot_of(axis, by, SUM1[p])], lambda by: s1_in[p].at[by]
        )

    cgrad[...] = lax.dot_general(
        dh[...], projection[...], (((1,), (1,)), ((), ())), preferred_element_type=F32
    ).astype(BF16)
    store = pltpu.make_async_copy(cgrad, cgrad_ref, last_sem.at[0])
    store.start()

    for p, (axis1, axis2, _) in enumerate(ORDERS):
        for copy in arrivals[p]:
            copy.wait_recv()
        value = s1_out[p][slot(axis1, SUM1[p]), :].astype(F32)
        for by in range(1, SIZE[axis1]):
            value += s1_in[p][by].astype(F32)
        s2_out[p][:SUM1[p], :] = value.astype(BF16)
        if FULL2[p] > SUM1[p]:
            s2_out[p][SUM1[p]:, :] = jnp.zeros((FULL2[p] - SUM1[p], LANES), BF16)
        arrivals[p] = start_all(
            1, p, axis2, lambda by: s2_out[p].at[slot_of(axis2, by, SUM2[p])], lambda by: s2_in[p].at[by]
        )

    for p, (_, axis2, axis3) in enumerate(ORDERS):
        for copy in arrivals[p]:
            copy.wait_recv()
        value = s2_out[p][slot(axis2, SUM2[p]), :].astype(F32)
        for by in range(1, SIZE[axis2]):
            value += s2_in[p][by].astype(F32)
        here = place(me, axis3)
        s3_in[p][here] = value.astype(BF16)
        arrivals[p] = start_all(2, p, axis3, lambda by: s3_in[p].at[here], lambda by: s3_in[p].at[here])

    devices = 1
    for size in SIZE.values():
        devices *= size

    for p, (_, axis2, axis3) in enumerate(ORDERS):
        for copy in arrivals[p]:
            copy.wait_recv()
        value = s3_in[p][0].astype(F32)
        for k in range(1, SIZE[axis3]):
            value += s3_in[p][k].astype(F32)
        mine = slot(axis2, SUM2[p])
        gather2[p][mine, :] = (value / devices).astype(BF16)
        arrivals[p] = start_all(3, p, axis2, lambda by: gather2[p].at[mine], lambda by: gather2[p].at[mine])

    for p, (axis1, _, _) in enumerate(ORDERS):
        for copy in arrivals[p]:
            copy.wait_recv()
        mine = slot(axis1, SUM1[p])
        gather1[p][mine, :] = gather2[p][:SUM1[p], :]
        arrivals[p] = start_all(4, p, axis1, lambda by: gather1[p].at[mine], lambda by: gather1[p].at[mine])

    writes = []
    for p in range(PARTS):
        for copy in arrivals[p]:
            copy.wait_recv()
        for j in range(COLS):
            result[p][:, j * LANES:(j + 1) * LANES] = gather1[p][j * PART[p]:(j + 1) * PART[p], :]
        dst = pgrad_ref.at[pl.ds(pl.multiple_of(core * HALF + FIRST[p], TILE), PART[p])]
        copy = remote(result[p], dst, last_send.at[p], last_recv.at[p], sibling)
        copy.start()
        write = pltpu.make_async_copy(result[p], dst, last_sem.at[1 + p])
        write.start()
        writes.append((copy, write))
    for copy, write in writes:
        copy.wait()
        write.wait()

    store.wait()
    for swap in [*swaps, swap_x, swap_core, *pending]:
        swap.wait_send()


def local(video_emb, captions, projection, labels, log_scale, bias):
    dma = pltpu.SemaphoreType.DMA
    vmem = pltpu.VMEM

    def each(shape_of, dtype=BF16):
        return [vmem(shape_of(p), dtype) for p in range(PARTS)]

    return pl.pallas_call(
        kernel,
        out_shape=(
            jax.ShapeDtypeStruct((ROWS, D), BF16),
            jax.ShapeDtypeStruct((D, E), BF16),
        ),
        in_specs=[pl.BlockSpec(memory_space=pltpu.HBM)] * 3
        + [pl.BlockSpec(memory_space=pltpu.VMEM)]
        + [pl.BlockSpec(memory_space=pltpu.SMEM)] * 2,
        out_specs=[pl.BlockSpec(memory_space=pltpu.HBM)] * 2,
        scratch_shapes=[
            vmem((ROWS, E), BF16),
            vmem((ROWS, D), BF16),
            vmem((D, E), BF16),
            vmem((D, ROWS), BF16),
            vmem((ROWS, E), F32),
            vmem((ROWS, E), BF16),
            vmem((ROWS, 1), F32),
            vmem((ROWS, E), F32),
            vmem((ROWS, E), BF16),
            vmem((ROWS, D), BF16),
            vmem((ROWS, E), BF16),
            vmem((ROWS, E), BF16),
            vmem((CHUNKS, 2 * CHUNK, E), BF16),
            each(lambda p: (FLAT[p], LANES)),
            each(lambda p: (FLAT[p], LANES)),
            each(lambda p: (FLAT[p], LANES), F32),
            each(lambda p: (FULL1[p], LANES)),
            each(lambda p: (SIZE[ORDERS[p][0]], SUM1[p], LANES)),
            each(lambda p: (FULL2[p], LANES)),
            each(lambda p: (SIZE[ORDERS[p][1]], SUM2[p], LANES)),
            each(lambda p: (SIZE[ORDERS[p][2]], SUM2[p], LANES)),
            each(lambda p: (FULL2[p], LANES)),
            each(lambda p: (FULL1[p], LANES)),
            each(lambda p: (PART[p], E)),
            dma((3,)),
            dma((4, CHUNKS)),
            dma((4, CHUNKS)),
            dma((PARTS,)),
            dma((PARTS,)),
            dma((5, PARTS, 8)),
            dma((5, PARTS, 8)),
            dma((1 + PARTS,)),
            dma((PARTS,)),
            dma((PARTS,)),
            pltpu.SemaphoreType.REGULAR,
        ],
        compiler_params=pltpu.CompilerParams(
            collective_id=0, has_side_effects=True, vmem_limit_bytes=63 << 20
        ),
    )(video_emb, captions, projection, labels, log_scale, bias)


def solution(mesh):
    return jax.shard_map(
        local,
        mesh=mesh,
        in_specs=(P("dp", None), P("dp", None), P(), P("dp"), P(), P()),
        out_specs=(P("dp", None), P()),
        check_vma=False,
    )
```

```python
import functools

import jax
import jax.numpy as jnp
from jax import lax
from jax.experimental import pallas as pl
from jax.experimental.pallas import tpu as pltpu
from jax.sharding import PartitionSpec as P

MESH = pl.DeviceIdType.MESH
F32 = jnp.float32
BF16 = jnp.bfloat16

AXES = {"core": (1, 2), "x": (2, 4), "z": (8, 8), "y": (64, 8)}
SIZE = {axis: size for axis, (_, size) in AXES.items()}

ROWS = 384
E = 640
D = 1152
HALF = D // 2
CHUNKS = 3
CHUNK = ROWS // CHUNKS
LANES = 128
COLS = E // LANES
TILE = 16

ORDERS = (("y", "z", "x"), ("z", "x", "y"), ("x", "y", "z"))
PART = (144, 144, 288)
FIRST = (0, 144, 288)
PARTS = len(ORDERS)


def up(value, multiple):
    return -(-value // multiple) * multiple


FLAT = tuple(rows * COLS for rows in PART)
SUM1 = tuple(up(-(-FLAT[p] // SIZE[ORDERS[p][0]]), TILE) for p in range(PARTS))
SUM2 = tuple(up(-(-SUM1[p] // SIZE[ORDERS[p][1]]), TILE) for p in range(PARTS))
FULL1 = tuple(SUM1[p] * SIZE[ORDERS[p][0]] for p in range(PARTS))
FULL2 = tuple(SUM2[p] * SIZE[ORDERS[p][1]] for p in range(PARTS))


def place(me, axis):
    stride, size = AXES[axis]
    return lax.rem(lax.div(me, stride), size)


def shifted(me, axis, by):
    stride, size = AXES[axis]
    here = place(me, axis)
    return me + (lax.rem(here + (by + size), size) - here) * stride


def remote(src, dst, send, recv, device):
    return pltpu.make_async_remote_copy(
        src_ref=src, dst_ref=dst, send_sem=send, recv_sem=recv, device_id=(device,), device_id_type=MESH
    )


def far_first(size):
    return sorted(range(1, size), key=lambda by: -min(by, size - by))


def far_last(size):
    return far_first(size)[::-1]


def kernel(
    video_ref, captions_ref, projection_ref, labels_ref, log_scale_ref, bias_ref,
    cgrad_ref, pgrad_ref,
    video, captions, projection, flipped, labels, zf, zc, inv, dz, dh,
    own_core, own_x, pool,
    out_core, in_core, own_term, s1_out, s1_in, s2_out, s2_in, s3_in, gather2, gather1, other1,
    load_sem, swap_send, swap_recv, core_send, core_recv,
    stage_send, stage_recv, last_send, last_recv, round_sem,
):
    me = lax.axis_index("dp")
    core = place(me, "core")
    sibling = shifted(me, "core", 1)

    loads = [
        pltpu.make_async_copy(video_ref, video, load_sem.at[0]),
        pltpu.make_async_copy(captions_ref, captions, load_sem.at[1]),
        pltpu.make_async_copy(projection_ref, projection, load_sem.at[2]),
        pltpu.make_async_copy(labels_ref, labels, load_sem.at[3]),
    ]
    for load in loads:
        load.start()

    barrier = pltpu.get_barrier_semaphore()
    greeted = [(axis, SIZE[axis] // 2) for axis in ("y", "z", "x")]
    greeted += [(axis, by) for axis in ("y", "z", "x") for by in (1, -1)] + [("core", 1)]
    for axis, by in greeted:
        pl.semaphore_signal(barrier, inc=1, device_id=(shifted(me, axis, by),), device_id_type=MESH)
    pl.semaphore_wait(barrier, len(greeted))
    loads[0].wait()

    swaps = []
    for q in range(CHUNKS):
        rows = pl.ds(q * CHUNK, CHUNK)
        for w, axis in enumerate(("y", "z")):
            swap = remote(
                video.at[rows], pool.at[q, pl.ds(w * CHUNK, CHUNK)], swap_send.at[w, q], swap_recv.at[w, q],
                shifted(me, axis, SIZE[axis] // 2),
            )
            swap.start()
            swaps.append(swap)
        if q == 0:
            swap_x = remote(video, own_x, swap_send.at[2, 0], swap_recv.at[2, 0], shifted(me, "x", SIZE["x"] // 2))
            swap_x.start()
            swap_core = remote(video, own_core, swap_send.at[3, 0], swap_recv.at[3, 0], sibling)
            swap_core.start()

    neighbours = [("y", 1), ("y", -1), ("z", 1), ("z", -1)]
    for axis, by in neighbours:
        pl.semaphore_signal(round_sem, inc=1, device_id=(shifted(me, axis, by),), device_id_type=MESH)

    scale = jnp.exp(jnp.full((1, 1), log_scale_ref[0], F32))
    shift = bias_ref[0]

    loads[1].wait()
    loads[2].wait()
    loads[3].wait()
    hidden = jnp.dot(captions[...], projection[...], preferred_element_type=F32)
    inverse = lax.rsqrt(jnp.sum(hidden * hidden, axis=-1, keepdims=True) + 1e-06)
    unit = hidden * inverse
    zf[...] = unit
    zc[...] = unit.astype(BF16)
    inv[...] = inverse

    def pairing(rows, sign=None):
        raw = rows.astype(F32)
        zv = (raw * lax.rsqrt(jnp.sum(raw * raw, axis=-1, keepdims=True) + 1e-06)).astype(BF16)
        logits = scale * lax.dot_general(
            zc[...], zv, (((1,), (1,)), ((), ())), preferred_element_type=F32
        ) + shift
        if sign is None:
            weight = 1.0 / (1.0 + jnp.exp(-logits))
        else:
            weight = sign / (1.0 + jnp.exp(-sign * logits))
        return jnp.dot(weight.astype(BF16), zv, preferred_element_type=F32)

    row = lax.broadcasted_iota(jnp.int32, (ROWS, ROWS), 0)
    column = lax.broadcasted_iota(jnp.int32, (ROWS, ROWS), 1)
    sign = jnp.where((row == column) & (labels[...].reshape(1, ROWS) == 1), -1.0, 1.0).astype(F32)
    dz[...] = pairing(video[...], sign)
    flipped[...] = captions[...].T
    pl.semaphore_wait(round_sem, len(neighbours))
    swap_core.wait_recv()
    dz[...] += pairing(own_core[...])
    swap_x.wait_recv()
    dz[...] += pairing(own_x[...])
    for q in range(CHUNKS):
        for swap in swaps[2 * q:2 * q + 2]:
            swap.wait_recv()
        dz[...] += pairing(pool[q])

    total = scale * dz[...]
    along = jnp.sum(zf[...] * total, axis=-1, keepdims=True)
    dh[...] = (inv[...] * (total - zf[...] * along)).astype(BF16)

    def term(half, part):
        rows = pl.ds(pl.multiple_of(half * HALF + FIRST[part], TILE), PART[part])
        return jnp.dot(flipped[rows, :], dh[...], preferred_element_type=F32)

    to_core = []
    for p in range(PARTS):
        value = term(1 - core, p).astype(BF16)
        for j in range(COLS):
            out_core[p][j * PART[p]:(j + 1) * PART[p], :] = value[:, j * LANES:(j + 1) * LANES]
        copy = remote(out_core[p], in_core[p], core_send.at[p], core_recv.at[p], sibling)
        copy.start()
        to_core.append(copy)
    for p in range(PARTS):
        value = term(core, p)
        for j in range(COLS):
            own_term[p][j * PART[p]:(j + 1) * PART[p], :] = value[:, j * LANES:(j + 1) * LANES]

    pending = list(to_core)

    def start_all(stage, p, axis, src_of, dst_of):
        copies = []
        for by in far_first(SIZE[axis]):
            copy = remote(
                src_of(by), dst_of(by), stage_send.at[stage, p, by], stage_recv.at[stage, p, by], shifted(me, axis, by)
            )
            copy.start()
            copies.append(copy)
        pending.extend(copies)
        return copies

    def slot(axis, rows):
        return pl.ds(pl.multiple_of(place(me, axis) * rows, TILE), rows)

    def slot_of(axis, by, rows):
        return pl.ds(pl.multiple_of(lax.rem(place(me, axis) + by, SIZE[axis]) * rows, TILE), rows)

    arrivals = [None] * PARTS
    for p, (axis, _, _) in enumerate(ORDERS):
        to_core[p].wait_recv()
        s1_out[p][:FLAT[p], :] = (own_term[p][...] + in_core[p][...].astype(F32)).astype(BF16)
        if FULL1[p] > FLAT[p]:
            s1_out[p][FLAT[p]:, :] = jnp.zeros((FULL1[p] - FLAT[p], LANES), BF16)
        arrivals[p] = start_all(
            0, p, axis, lambda by: s1_out[p].at[slot_of(axis, by, SUM1[p])], lambda by: s1_in[p].at[by]
        )

    cgrad_ref[...] = lax.dot_general(
        dh[...], projection[...], (((1,), (1,)), ((), ())), preferred_element_type=F32
    ).astype(BF16)

    for p, (axis1, axis2, _) in enumerate(ORDERS):
        for copy in arrivals[p]:
            copy.wait_recv()
        value = s1_out[p][slot(axis1, SUM1[p]), :].astype(F32)
        for by in range(1, SIZE[axis1]):
            value += s1_in[p][by].astype(F32)
        s2_out[p][:SUM1[p], :] = value.astype(BF16)
        if FULL2[p] > SUM1[p]:
            s2_out[p][SUM1[p]:, :] = jnp.zeros((FULL2[p] - SUM1[p], LANES), BF16)
        arrivals[p] = start_all(
            1, p, axis2, lambda by: s2_out[p].at[slot_of(axis2, by, SUM2[p])], lambda by: s2_in[p].at[by]
        )

    for p, (_, axis2, axis3) in enumerate(ORDERS):
        for copy in arrivals[p]:
            copy.wait_recv()
        value = s2_out[p][slot(axis2, SUM2[p]), :].astype(F32)
        for by in range(1, SIZE[axis2]):
            value += s2_in[p][by].astype(F32)
        here = place(me, axis3)
        s3_in[p][here] = value.astype(BF16)
        arrivals[p] = start_all(2, p, axis3, lambda by: s3_in[p].at[here], lambda by: s3_in[p].at[here])

    devices = 1
    for size in SIZE.values():
        devices *= size

    for p, (_, axis2, axis3) in enumerate(ORDERS):
        for copy in arrivals[p]:
            copy.wait_recv()
        value = s3_in[p][0].astype(F32)
        for k in range(1, SIZE[axis3]):
            value += s3_in[p][k].astype(F32)
        mine = slot(axis2, SUM2[p])
        gather2[p][mine, :] = (value / devices).astype(BF16)
        arrivals[p] = start_all(3, p, axis2, lambda by: gather2[p].at[mine], lambda by: gather2[p].at[mine])

    crossings = [[] for _ in range(PARTS)]

    def across(p, by):
        axis = ORDERS[p][0]
        rows = slot_of(axis, SIZE[axis] - by, SUM1[p])
        copy = remote(gather1[p].at[rows], other1[p].at[rows], last_send.at[p, by], last_recv.at[p, by], sibling)
        copy.start()
        crossings[p].append(copy)

    for p, (axis1, _, _) in enumerate(ORDERS):
        for copy in arrivals[p]:
            copy.wait_recv()
        mine = slot(axis1, SUM1[p])
        gather1[p][mine, :] = gather2[p][:SUM1[p], :]
        arrivals[p] = start_all(4, p, axis1, lambda by: gather1[p].at[mine], lambda by: gather1[p].at[mine])
        across(p, 0)

    for p, (axis1, _, _) in enumerate(ORDERS):
        for by, copy in zip(far_last(SIZE[axis1]), reversed(arrivals[p])):
            copy.wait_recv()
            across(p, by)
    for p in range(PARTS):
        for j in range(COLS):
            rows = pl.ds(pl.multiple_of(core * HALF + FIRST[p], TILE), PART[p])
            pgrad_ref[rows, j * LANES:(j + 1) * LANES] = gather1[p][j * PART[p]:(j + 1) * PART[p], :]
    for p in range(PARTS):
        for copy in crossings[p]:
            copy.wait_recv()
        for j in range(COLS):
            rows = pl.ds(pl.multiple_of((1 - core) * HALF + FIRST[p], TILE), PART[p])
            pgrad_ref[rows, j * LANES:(j + 1) * LANES] = other1[p][j * PART[p]:(j + 1) * PART[p], :]
        pending.extend(crossings[p])

    for swap in [*swaps, swap_x, swap_core, *pending]:
        swap.wait_send()


def hand_over(cgrad_ref, pgrad_ref, cgrad_out, pgrad_out, sem):
    copies = [
        pltpu.make_async_copy(cgrad_ref, cgrad_out, sem.at[0]),
        pltpu.make_async_copy(pgrad_ref, pgrad_out, sem.at[1]),
    ]
    for copy in copies:
        copy.start()
    for copy in copies:
        copy.wait()


def local(video_emb, captions, projection, labels, log_scale, bias):
    dma = pltpu.SemaphoreType.DMA
    vmem = pltpu.VMEM

    def each(shape_of, dtype=BF16):
        return [vmem(shape_of(p), dtype) for p in range(PARTS)]

    held = [pltpu.with_memory_space_constraint(x, pltpu.HBM) for x in (video_emb, captions, projection, labels)]
    cgrad, pgrad = pl.pallas_call(
        kernel,
        out_shape=(
            jax.ShapeDtypeStruct((ROWS, D), BF16),
            jax.ShapeDtypeStruct((D, E), BF16),
        ),
        in_specs=[pl.BlockSpec(memory_space=pl.ANY)] * 4
        + [pl.BlockSpec(memory_space=pltpu.SMEM)] * 2,
        out_specs=[pl.BlockSpec(memory_space=pltpu.VMEM)] * 2,
        scratch_shapes=[
            vmem((ROWS, E), BF16),
            vmem((ROWS, D), BF16),
            vmem((D, E), BF16),
            vmem((D, ROWS), BF16),
            vmem((ROWS,), jnp.int32),
            vmem((ROWS, E), F32),
            vmem((ROWS, E), BF16),
            vmem((ROWS, 1), F32),
            vmem((ROWS, E), F32),
            vmem((ROWS, E), BF16),
            vmem((ROWS, E), BF16),
            vmem((ROWS, E), BF16),
            vmem((CHUNKS, 2 * CHUNK, E), BF16),
            each(lambda p: (FLAT[p], LANES)),
            each(lambda p: (FLAT[p], LANES)),
            each(lambda p: (FLAT[p], LANES), F32),
            each(lambda p: (FULL1[p], LANES)),
            each(lambda p: (SIZE[ORDERS[p][0]], SUM1[p], LANES)),
            each(lambda p: (FULL2[p], LANES)),
            each(lambda p: (SIZE[ORDERS[p][1]], SUM2[p], LANES)),
            each(lambda p: (SIZE[ORDERS[p][2]], SUM2[p], LANES)),
            each(lambda p: (FULL2[p], LANES)),
            each(lambda p: (FULL1[p], LANES)),
            each(lambda p: (FULL1[p], LANES)),
            dma((4,)),
            dma((4, CHUNKS)),
            dma((4, CHUNKS)),
            dma((PARTS,)),
            dma((PARTS,)),
            dma((5, PARTS, 8)),
            dma((5, PARTS, 8)),
            dma((PARTS, 8)),
            dma((PARTS, 8)),
            pltpu.SemaphoreType.REGULAR,
        ],
        compiler_params=pltpu.CompilerParams(
            collective_id=0, has_side_effects=True, vmem_limit_bytes=40 << 20
        ),
    )(*held, log_scale, bias)
    return pl.pallas_call(
        hand_over,
        out_shape=(
            jax.ShapeDtypeStruct((ROWS, D), BF16),
            jax.ShapeDtypeStruct((D, E), BF16),
        ),
        in_specs=[pl.BlockSpec(memory_space=pl.ANY)] * 2,
        out_specs=[pl.BlockSpec(memory_space=pl.ANY)] * 2,
        scratch_shapes=[dma((2,))],
    )(cgrad, pgrad)


def solution(mesh):
    return jax.shard_map(
        local,
        mesh=mesh,
        in_specs=(P("dp", None), P("dp", None), P(), P("dp"), P(), P()),
        out_specs=(P("dp", None), P()),
        check_vma=False,
    )
```

```python
import functools

import jax
import jax.numpy as jnp
from jax import lax
from jax.experimental import pallas as pl
from jax.experimental.pallas import tpu as pltpu
from jax.sharding import PartitionSpec as P

MESH = pl.DeviceIdType.MESH
F32 = jnp.float32
BF16 = jnp.bfloat16

AXES = {"core": (1, 2), "x": (2, 4), "z": (8, 8), "y": (64, 8)}
SIZE = {axis: size for axis, (_, size) in AXES.items()}

ROWS = 384
E = 640
D = 1152
HALF = D // 2
CHUNKS = 3
CHUNK = ROWS // CHUNKS
LANES = 128
COLS = E // LANES
TILE = 16

ORDERS = (("x", "y", "z"), ("y", "z", "x"), ("z", "x", "y"))
PART = (288, 144, 144)
FIRST = (0, 288, 432)
PARTS = len(ORDERS)
PIECES = 3


def up(value, multiple):
    return -(-value // multiple) * multiple


FLAT = tuple(rows * COLS for rows in PART)
SUM1 = tuple(up(-(-FLAT[p] // SIZE[ORDERS[p][0]]), TILE) for p in range(PARTS))
SUM2 = tuple(up(-(-SUM1[p] // SIZE[ORDERS[p][1]]), TILE) for p in range(PARTS))
FULL1 = tuple(SUM1[p] * SIZE[ORDERS[p][0]] for p in range(PARTS))
FULL2 = tuple(SUM2[p] * SIZE[ORDERS[p][1]] for p in range(PARTS))


def place(me, axis):
    stride, size = AXES[axis]
    return lax.rem(lax.div(me, stride), size)


def shifted(me, axis, by):
    stride, size = AXES[axis]
    here = place(me, axis)
    return me + (lax.rem(here + (by + size), size) - here) * stride


def remote(src, dst, send, recv, device):
    return pltpu.make_async_remote_copy(
        src_ref=src, dst_ref=dst, send_sem=send, recv_sem=recv, device_id=(device,), device_id_type=MESH
    )


def far_first(size):
    return sorted(range(1, size), key=lambda by: -min(by, size - by))


def far_last(size):
    return far_first(size)[::-1]


def kernel(
    video_ref, captions_ref, projection_ref, labels_ref, log_scale_ref, bias_ref,
    cgrad_ref, pgrad_ref,
    video, captions, projection, flipped, labels, zf, zc, inv, dz, dh,
    own_core, own_x, pool,
    out_core, in_core, own_term, s1_out, s1_in, s2_out, s2_in, s3_in, gather2, gather1, other1,
    load_sem, swap_send, swap_recv, core_send, core_recv,
    stage_send, stage_recv, last_send, last_recv, round_sem,
):
    me = lax.axis_index("dp")
    core = place(me, "core")
    sibling = shifted(me, "core", 1)

    loads = [
        pltpu.make_async_copy(video_ref, video, load_sem.at[0]),
        pltpu.make_async_copy(captions_ref, captions, load_sem.at[1]),
        pltpu.make_async_copy(projection_ref, projection, load_sem.at[2]),
        pltpu.make_async_copy(labels_ref, labels, load_sem.at[3]),
    ]
    for load in loads:
        load.start()

    barrier = pltpu.get_barrier_semaphore()
    greeted = [(axis, SIZE[axis] // 2) for axis in ("y", "z", "x")]
    greeted += [(axis, by) for axis in ("y", "z", "x") for by in (1, -1)] + [("core", 1)]
    for axis, by in greeted:
        pl.semaphore_signal(barrier, inc=1, device_id=(shifted(me, axis, by),), device_id_type=MESH)
    pl.semaphore_wait(barrier, len(greeted))
    loads[0].wait()

    swaps = []
    for q in range(CHUNKS):
        rows = pl.ds(q * CHUNK, CHUNK)
        for w, axis in enumerate(("y", "z")):
            swap = remote(
                video.at[rows], pool.at[q, pl.ds(w * CHUNK, CHUNK)], swap_send.at[w, q], swap_recv.at[w, q],
                shifted(me, axis, SIZE[axis] // 2),
            )
            swap.start()
            swaps.append(swap)
        if q == 0:
            swap_x = remote(video, own_x, swap_send.at[2, 0], swap_recv.at[2, 0], shifted(me, "x", SIZE["x"] // 2))
            swap_x.start()
            swap_core = remote(video, own_core, swap_send.at[3, 0], swap_recv.at[3, 0], sibling)
            swap_core.start()

    neighbours = [("y", 1), ("y", -1), ("z", 1), ("z", -1)]
    for axis, by in neighbours:
        pl.semaphore_signal(round_sem, inc=1, device_id=(shifted(me, axis, by),), device_id_type=MESH)

    scale = jnp.exp(jnp.full((1, 1), log_scale_ref[0], F32))
    shift = bias_ref[0]

    loads[1].wait()
    loads[2].wait()
    loads[3].wait()
    hidden = jnp.dot(captions[...], projection[...], preferred_element_type=F32)
    inverse = lax.rsqrt(jnp.sum(hidden * hidden, axis=-1, keepdims=True) + 1e-06)
    unit = hidden * inverse
    zf[...] = unit
    zc[...] = unit.astype(BF16)
    inv[...] = inverse

    def pairing(rows, sign=None):
        raw = rows.astype(F32)
        zv = (raw * lax.rsqrt(jnp.sum(raw * raw, axis=-1, keepdims=True) + 1e-06)).astype(BF16)
        logits = scale * lax.dot_general(
            zc[...], zv, (((1,), (1,)), ((), ())), preferred_element_type=F32
        ) + shift
        if sign is None:
            weight = 1.0 / (1.0 + jnp.exp(-logits))
        else:
            weight = sign / (1.0 + jnp.exp(-sign * logits))
        return jnp.dot(weight.astype(BF16), zv, preferred_element_type=F32)

    row = lax.broadcasted_iota(jnp.int32, (ROWS, ROWS), 0)
    column = lax.broadcasted_iota(jnp.int32, (ROWS, ROWS), 1)
    sign = jnp.where((row == column) & (labels[...].reshape(1, ROWS) == 1), -1.0, 1.0).astype(F32)
    dz[...] = pairing(video[...], sign)
    flipped[...] = captions[...].T
    pl.semaphore_wait(round_sem, len(neighbours))
    swap_core.wait_recv()
    dz[...] += pairing(own_core[...])
    swap_x.wait_recv()
    dz[...] += pairing(own_x[...])
    for q in range(CHUNKS):
        for swap in swaps[2 * q:2 * q + 2]:
            swap.wait_recv()
        dz[...] += pairing(pool[q])

    total = scale * dz[...]
    along = jnp.sum(zf[...] * total, axis=-1, keepdims=True)
    dh[...] = (inv[...] * (total - zf[...] * along)).astype(BF16)

    def term(half, part):
        rows = pl.ds(pl.multiple_of(half * HALF + FIRST[part], TILE), PART[part])
        return jnp.dot(flipped[rows, :], dh[...], preferred_element_type=F32)

    to_core = []
    for p in range(PARTS):
        value = term(1 - core, p).astype(BF16)
        for j in range(COLS):
            out_core[p][j * PART[p]:(j + 1) * PART[p], :] = value[:, j * LANES:(j + 1) * LANES]
        copy = remote(out_core[p], in_core[p], core_send.at[p], core_recv.at[p], sibling)
        copy.start()
        to_core.append(copy)
    for p in range(PARTS):
        value = term(core, p)
        for j in range(COLS):
            own_term[p][j * PART[p]:(j + 1) * PART[p], :] = value[:, j * LANES:(j + 1) * LANES]

    pending = [*swaps, swap_x, swap_core, *to_core]

    def sent():
        for copy in pending:
            copy.wait_send()
        pending[:] = started
        started.clear()

    started = []

    def start_all(stage, p, axis, src_of, dst_of):
        copies = []
        for by in far_first(SIZE[axis]):
            copy = remote(
                src_of(by), dst_of(by), stage_send.at[stage, p, by], stage_recv.at[stage, p, by], shifted(me, axis, by)
            )
            copy.start()
            copies.append(copy)
        started.extend(copies)
        return copies

    def slot(axis, rows):
        return pl.ds(pl.multiple_of(place(me, axis) * rows, TILE), rows)

    def slot_of(axis, by, rows):
        return pl.ds(pl.multiple_of(lax.rem(place(me, axis) + by, SIZE[axis]) * rows, TILE), rows)

    arrivals = [None] * PARTS
    for p, (axis, _, _) in enumerate(ORDERS):
        to_core[p].wait_recv()
        s1_out[p][:FLAT[p], :] = (own_term[p][...] + in_core[p][...].astype(F32)).astype(BF16)
        if FULL1[p] > FLAT[p]:
            s1_out[p][FLAT[p]:, :] = jnp.zeros((FULL1[p] - FLAT[p], LANES), BF16)
        arrivals[p] = start_all(
            0, p, axis, lambda by: s1_out[p].at[slot_of(axis, by, SUM1[p])], lambda by: s1_in[p].at[by]
        )

    cgrad_ref[...] = lax.dot_general(
        dh[...], projection[...], (((1,), (1,)), ((), ())), preferred_element_type=F32
    ).astype(BF16)

    sent()

    for p, (axis1, axis2, _) in enumerate(ORDERS):
        for copy in arrivals[p]:
            copy.wait_recv()
        value = s1_out[p][slot(axis1, SUM1[p]), :].astype(F32)
        for by in range(1, SIZE[axis1]):
            value += s1_in[p][by].astype(F32)
        s2_out[p][:SUM1[p], :] = value.astype(BF16)
        if FULL2[p] > SUM1[p]:
            s2_out[p][SUM1[p]:, :] = jnp.zeros((FULL2[p] - SUM1[p], LANES), BF16)
        arrivals[p] = start_all(
            1, p, axis2, lambda by: s2_out[p].at[slot_of(axis2, by, SUM2[p])], lambda by: s2_in[p].at[by]
        )

    sent()

    for p, (_, axis2, axis3) in enumerate(ORDERS):
        for copy in arrivals[p]:
            copy.wait_recv()
        value = s2_out[p][slot(axis2, SUM2[p]), :].astype(F32)
        for by in range(1, SIZE[axis2]):
            value += s2_in[p][by].astype(F32)
        here = place(me, axis3)
        s3_in[p][here] = value.astype(BF16)
        arrivals[p] = start_all(2, p, axis3, lambda by: s3_in[p].at[here], lambda by: s3_in[p].at[here])

    devices = 1
    for size in SIZE.values():
        devices *= size

    sent()

    for p, (_, axis2, axis3) in enumerate(ORDERS):
        for copy in arrivals[p]:
            copy.wait_recv()
        value = s3_in[p][0].astype(F32)
        for k in range(1, SIZE[axis3]):
            value += s3_in[p][k].astype(F32)
        mine = slot(axis2, SUM2[p])
        gather2[p][mine, :] = (value / devices).astype(BF16)
        arrivals[p] = start_all(3, p, axis2, lambda by: gather2[p].at[mine], lambda by: gather2[p].at[mine])

    crossings = [[] for _ in range(PARTS)]

    def across(p, by):
        axis = ORDERS[p][0]
        rows = slot_of(axis, SIZE[axis] - by, SUM1[p])
        copy = remote(gather1[p].at[rows], other1[p].at[rows], last_send.at[p, by], last_recv.at[p, by], sibling)
        copy.start()
        crossings[p].append(copy)

    sent()

    for p, (axis1, _, _) in enumerate(ORDERS):
        for copy in arrivals[p]:
            copy.wait_recv()
        mine = slot(axis1, SUM1[p])
        gather1[p][mine, :] = gather2[p][:SUM1[p], :]
        arrivals[p] = start_all(4, p, axis1, lambda by: gather1[p].at[mine], lambda by: gather1[p].at[mine])
        across(p, 0)

    sent()

    for p, (axis1, _, _) in enumerate(ORDERS):
        for by, copy in zip(far_last(SIZE[axis1]), reversed(arrivals[p])):
            copy.wait_recv()
            across(p, by)
    for p in range(PARTS):
        for j in range(COLS):
            rows = pl.ds(pl.multiple_of(core * HALF + FIRST[p], TILE), PART[p])
            pgrad_ref[rows, j * LANES:(j + 1) * LANES] = gather1[p][j * PART[p]:(j + 1) * PART[p], :]
    for p in range(PARTS):
        for copy in crossings[p]:
            copy.wait_recv()
        for j in range(COLS):
            rows = pl.ds(pl.multiple_of((1 - core) * HALF + FIRST[p], TILE), PART[p])
            pgrad_ref[rows, j * LANES:(j + 1) * LANES] = other1[p][j * PART[p]:(j + 1) * PART[p], :]
        started.extend(crossings[p])

    sent()
    sent()


def hand_over(cgrad_ref, pgrad_ref, cgrad_out, pgrad_out, sem):
    copies = []
    for source, target in ((cgrad_ref, cgrad_out), (pgrad_ref, pgrad_out)):
        rows = source.shape[0] // PIECES
        for k in range(PIECES):
            piece = pl.ds(k * rows, rows)
            copies.append(pltpu.make_async_copy(source.at[piece], target.at[piece], sem.at[len(copies)]))
    for copy in copies:
        copy.start()
    for copy in copies:
        copy.wait()


def local(video_emb, captions, projection, labels, log_scale, bias):
    dma = pltpu.SemaphoreType.DMA
    vmem = pltpu.VMEM

    def each(shape_of, dtype=BF16):
        return [vmem(shape_of(p), dtype) for p in range(PARTS)]

    held = [pltpu.with_memory_space_constraint(x, pltpu.HBM) for x in (video_emb, captions, projection, labels)]
    cgrad, pgrad = pl.pallas_call(
        kernel,
        out_shape=(
            jax.ShapeDtypeStruct((ROWS, D), BF16),
            jax.ShapeDtypeStruct((D, E), BF16),
        ),
        in_specs=[pl.BlockSpec(memory_space=pl.ANY)] * 4
        + [pl.BlockSpec(memory_space=pltpu.SMEM)] * 2,
        out_specs=[pl.BlockSpec(memory_space=pltpu.VMEM)] * 2,
        scratch_shapes=[
            vmem((ROWS, E), BF16),
            vmem((ROWS, D), BF16),
            vmem((D, E), BF16),
            vmem((D, ROWS), BF16),
            vmem((ROWS,), jnp.int32),
            vmem((ROWS, E), F32),
            vmem((ROWS, E), BF16),
            vmem((ROWS, 1), F32),
            vmem((ROWS, E), F32),
            vmem((ROWS, E), BF16),
            vmem((ROWS, E), BF16),
            vmem((ROWS, E), BF16),
            vmem((CHUNKS, 2 * CHUNK, E), BF16),
            each(lambda p: (FLAT[p], LANES)),
            each(lambda p: (FLAT[p], LANES)),
            each(lambda p: (FLAT[p], LANES), F32),
            each(lambda p: (FULL1[p], LANES)),
            each(lambda p: (SIZE[ORDERS[p][0]], SUM1[p], LANES)),
            each(lambda p: (FULL2[p], LANES)),
            each(lambda p: (SIZE[ORDERS[p][1]], SUM2[p], LANES)),
            each(lambda p: (SIZE[ORDERS[p][2]], SUM2[p], LANES)),
            each(lambda p: (FULL2[p], LANES)),
            each(lambda p: (FULL1[p], LANES)),
            each(lambda p: (FULL1[p], LANES)),
            dma((4,)),
            dma((4, CHUNKS)),
            dma((4, CHUNKS)),
            dma((PARTS,)),
            dma((PARTS,)),
            dma((5, PARTS, 8)),
            dma((5, PARTS, 8)),
            dma((PARTS, 8)),
            dma((PARTS, 8)),
            pltpu.SemaphoreType.REGULAR,
        ],
        compiler_params=pltpu.CompilerParams(
            collective_id=0, has_side_effects=True, vmem_limit_bytes=40 << 20
        ),
    )(*held, log_scale, bias)
    return pl.pallas_call(
        hand_over,
        out_shape=(
            jax.ShapeDtypeStruct((ROWS, D), BF16),
            jax.ShapeDtypeStruct((D, E), BF16),
        ),
        in_specs=[pl.BlockSpec(memory_space=pl.ANY)] * 2,
        out_specs=[pl.BlockSpec(memory_space=pl.ANY)] * 2,
        scratch_shapes=[dma((2 * PIECES,))],
        compiler_params=pltpu.CompilerParams(vmem_limit_bytes=1 << 20),
    )(cgrad, pgrad)


def solution(mesh):
    return jax.shard_map(
        local,
        mesh=mesh,
        in_specs=(P("dp", None), P("dp", None), P(), P("dp"), P(), P()),
        out_specs=(P("dp", None), P()),
        check_vma=False,
    )
```

```python
import functools

import jax
import jax.numpy as jnp
from jax import lax
from jax.experimental import pallas as pl
from jax.experimental.pallas import tpu as pltpu
from jax.sharding import PartitionSpec as P

MESH = pl.DeviceIdType.MESH
F32 = jnp.float32
BF16 = jnp.bfloat16

AXES = {"core": (1, 2), "x": (2, 4), "z": (8, 8), "y": (64, 8)}
SIZE = {axis: size for axis, (_, size) in AXES.items()}

ROWS = 384
E = 640
D = 1152
HALF = D // 2
CHUNKS = 3
CHUNK = ROWS // (2 * CHUNKS)
NEAR, REST = 1, 3
WAYS = (("y", 1), ("y", -1), ("z", 1), ("z", -1))
LANES = 128
COLS = E // LANES
TILE = 16

ORDERS = (("x", "y", "z"), ("y", "x", "z"), ("z", "x", "y"))
PART = (256, 160, 160)
FIRST = (0, 256, 416)
PARTS = len(ORDERS)
READY = (1, 2, 0)
PIECES = 3


def up(value, multiple):
    return -(-value // multiple) * multiple


FLAT = tuple(rows * COLS for rows in PART)
SUM1 = tuple(up(-(-FLAT[p] // SIZE[ORDERS[p][0]]), TILE) for p in range(PARTS))
SUM2 = tuple(up(-(-SUM1[p] // SIZE[ORDERS[p][1]]), TILE) for p in range(PARTS))
FULL1 = tuple(SUM1[p] * SIZE[ORDERS[p][0]] for p in range(PARTS))
FULL2 = tuple(SUM2[p] * SIZE[ORDERS[p][1]] for p in range(PARTS))


def place(me, axis):
    stride, size = AXES[axis]
    return lax.rem(lax.div(me, stride), size)


def shifted(me, axis, by):
    stride, size = AXES[axis]
    here = place(me, axis)
    return me + (lax.rem(here + (by + size), size) - here) * stride


def remote(src, dst, send, recv, device):
    return pltpu.make_async_remote_copy(
        src_ref=src, dst_ref=dst, send_sem=send, recv_sem=recv, device_id=(device,), device_id_type=MESH
    )


def far_first(size):
    return sorted(range(1, size), key=lambda by: -min(by, size - by))


def far_last(size):
    return far_first(size)[::-1]


def kernel(
    video_ref, captions_ref, projection_ref, labels_ref, log_scale_ref, bias_ref,
    cgrad_ref, pgrad_ref,
    video, captions, projection, flipped, labels, zf, zc, inv, dz, dh,
    own_core, own_x, relay, pool,
    out_core, in_core, own_term, s1_out, s1_in, s2_out, s2_in, s3_in, gather2, gather1, other1,
    load_sem, hop_send, hop_recv, swap_send, swap_recv, core_send, core_recv,
    stage_send, stage_recv, last_send, last_recv, round_sem,
):
    me = lax.axis_index("dp")
    core = place(me, "core")
    sibling = shifted(me, "core", 1)

    loads = [
        pltpu.make_async_copy(video_ref, video, load_sem.at[0]),
        pltpu.make_async_copy(captions_ref, captions, load_sem.at[1]),
        pltpu.make_async_copy(projection_ref, projection, load_sem.at[2]),
        pltpu.make_async_copy(labels_ref, labels, load_sem.at[3]),
    ]
    for load in loads:
        load.start()

    barrier = pltpu.get_barrier_semaphore()
    greeted = [(axis, way * by) for by in sorted({1, NEAR, REST}) for axis, way in WAYS]
    greeted += [("x", 2), ("x", 1), ("x", -1), ("core", 1)]
    for axis, by in greeted:
        pl.semaphore_signal(barrier, inc=1, device_id=(shifted(me, axis, by),), device_id_type=MESH)
    pl.semaphore_wait(barrier, len(greeted))
    loads[0].wait()

    hops = []
    for q in range(CHUNKS):
        for w, (axis, way) in enumerate(WAYS):
            rows = pl.ds(((0 if way > 0 else CHUNKS) + q) * CHUNK, CHUNK)
            first = remote(
                video.at[rows], relay.at[q, w], hop_send.at[q, w, 0], hop_recv.at[q, w, 0], shifted(me, axis, way * NEAR)
            )
            second = remote(
                relay.at[q, w], pool.at[q, pl.ds(w * CHUNK, CHUNK)], hop_send.at[q, w, 1], hop_recv.at[q, w, 1],
                shifted(me, axis, way * REST),
            )
            first.start()
            hops.append((first, second))
    swap_x = remote(video, own_x, swap_send.at[0], swap_recv.at[0], shifted(me, "x", 2))
    swap_x.start()
    swap_core = remote(video, own_core, swap_send.at[1], swap_recv.at[1], sibling)
    swap_core.start()

    def pass_on(q):
        for first, second in hops[q * len(WAYS):(q + 1) * len(WAYS)]:
            first.wait_recv()
            second.start()

    neighbours = [("y", 1), ("y", -1), ("z", 1), ("z", -1)]
    for axis, by in neighbours:
        pl.semaphore_signal(round_sem, inc=1, device_id=(shifted(me, axis, by),), device_id_type=MESH)

    scale = jnp.exp(jnp.full((1, 1), log_scale_ref[0], F32))
    shift = bias_ref[0]

    loads[1].wait()
    loads[2].wait()
    loads[3].wait()
    hidden = jnp.dot(captions[...], projection[...], preferred_element_type=F32)
    inverse = lax.rsqrt(jnp.sum(hidden * hidden, axis=-1, keepdims=True) + 1e-06)
    unit = hidden * inverse
    zf[...] = unit
    zc[...] = unit.astype(BF16)
    inv[...] = inverse

    def pairing(rows, sign=None):
        raw = rows.astype(F32)
        zv = (raw * lax.rsqrt(jnp.sum(raw * raw, axis=-1, keepdims=True) + 1e-06)).astype(BF16)
        logits = scale * lax.dot_general(
            zc[...], zv, (((1,), (1,)), ((), ())), preferred_element_type=F32
        ) + shift
        if sign is None:
            weight = 1.0 / (1.0 + jnp.exp(-logits))
        else:
            weight = sign / (1.0 + jnp.exp(-sign * logits))
        return jnp.dot(weight.astype(BF16), zv, preferred_element_type=F32)

    pass_on(0)
    row = lax.broadcasted_iota(jnp.int32, (ROWS, ROWS), 0)
    column = lax.broadcasted_iota(jnp.int32, (ROWS, ROWS), 1)
    sign = jnp.where((row == column) & (labels[...].reshape(1, ROWS) == 1), -1.0, 1.0).astype(F32)
    dz[...] = pairing(video[...], sign)
    for q in range(1, CHUNKS):
        pass_on(q)
    flipped[...] = captions[...].T
    pl.semaphore_wait(round_sem, len(neighbours))
    swap_core.wait_recv()
    dz[...] += pairing(own_core[...])
    swap_x.wait_recv()
    dz[...] += pairing(own_x[...])
    for q in range(CHUNKS):
        for _, second in hops[q * len(WAYS):(q + 1) * len(WAYS)]:
            second.wait_recv()
        if q < CHUNKS - 1:
            dz[...] += pairing(pool[q])

    total = scale * (dz[...] + pairing(pool[CHUNKS - 1]))
    along = jnp.sum(zf[...] * total, axis=-1, keepdims=True)
    dh[...] = (inv[...] * (total - zf[...] * along)).astype(BF16)

    def term(half, part):
        rows = pl.ds(pl.multiple_of(half * HALF + FIRST[part], TILE), PART[part])
        return jnp.dot(flipped[rows, :], dh[...], preferred_element_type=F32)

    to_core = []
    for p in range(PARTS):
        value = term(1 - core, p).astype(BF16)
        for j in range(COLS):
            out_core[p][j * PART[p]:(j + 1) * PART[p], :] = value[:, j * LANES:(j + 1) * LANES]
        copy = remote(out_core[p], in_core[p], core_send.at[p], core_recv.at[p], sibling)
        copy.start()
        to_core.append(copy)
    for p in range(PARTS):
        value = term(core, p)
        for j in range(COLS):
            own_term[p][j * PART[p]:(j + 1) * PART[p], :] = value[:, j * LANES:(j + 1) * LANES]

    pending = [copy for pair in hops for copy in pair] + [swap_x, swap_core, *to_core]

    def sent():
        for copy in pending:
            copy.wait_send()
        pending[:] = started
        started.clear()

    started = []

    def start_all(stage, p, axis, src_of, dst_of):
        copies = []
        for by in far_first(SIZE[axis]):
            copy = remote(
                src_of(by), dst_of(by), stage_send.at[stage, p, by], stage_recv.at[stage, p, by], shifted(me, axis, by)
            )
            copy.start()
            copies.append(copy)
        started.extend(copies)
        return copies

    def slot(axis, rows):
        return pl.ds(pl.multiple_of(place(me, axis) * rows, TILE), rows)

    def slot_of(axis, by, rows):
        return pl.ds(pl.multiple_of(lax.rem(place(me, axis) + by, SIZE[axis]) * rows, TILE), rows)

    arrivals = [None] * PARTS
    for p, (axis, _, _) in enumerate(ORDERS):
        to_core[p].wait_recv()
        s1_out[p][:FLAT[p], :] = (own_term[p][...] + in_core[p][...].astype(F32)).astype(BF16)
        if FULL1[p] > FLAT[p]:
            s1_out[p][FLAT[p]:, :] = jnp.zeros((FULL1[p] - FLAT[p], LANES), BF16)
        arrivals[p] = start_all(
            0, p, axis, lambda by: s1_out[p].at[slot_of(axis, by, SUM1[p])], lambda by: s1_in[p].at[by]
        )

    cgrad_ref[...] = lax.dot_general(
        dh[...], projection[...], (((1,), (1,)), ((), ())), preferred_element_type=F32
    ).astype(BF16)

    sent()

    for p, (axis1, axis2, _) in enumerate(ORDERS):
        for copy in arrivals[p]:
            copy.wait_recv()
        value = s1_out[p][slot(axis1, SUM1[p]), :].astype(F32)
        for by in range(1, SIZE[axis1]):
            value += s1_in[p][by].astype(F32)
        s2_out[p][:SUM1[p], :] = value.astype(BF16)
        if FULL2[p] > SUM1[p]:
            s2_out[p][SUM1[p]:, :] = jnp.zeros((FULL2[p] - SUM1[p], LANES), BF16)
        arrivals[p] = start_all(
            1, p, axis2, lambda by: s2_out[p].at[slot_of(axis2, by, SUM2[p])], lambda by: s2_in[p].at[by]
        )

    sent()

    for p, (_, axis2, axis3) in enumerate(ORDERS):
        for copy in arrivals[p]:
            copy.wait_recv()
        value = s2_out[p][slot(axis2, SUM2[p]), :].astype(F32)
        for by in range(1, SIZE[axis2]):
            value += s2_in[p][by].astype(F32)
        here = place(me, axis3)
        s3_in[p][here] = value.astype(BF16)
        arrivals[p] = start_all(2, p, axis3, lambda by: s3_in[p].at[here], lambda by: s3_in[p].at[here])

    devices = 1
    for size in SIZE.values():
        devices *= size

    sent()

    for p, (_, axis2, axis3) in enumerate(ORDERS):
        for copy in arrivals[p]:
            copy.wait_recv()
        value = s3_in[p][0].astype(F32)
        for k in range(1, SIZE[axis3]):
            value += s3_in[p][k].astype(F32)
        mine = slot(axis2, SUM2[p])
        gather2[p][mine, :] = (value / devices).astype(BF16)
        arrivals[p] = start_all(3, p, axis2, lambda by: gather2[p].at[mine], lambda by: gather2[p].at[mine])

    crossings = [[] for _ in range(PARTS)]

    def across(p, by):
        axis = ORDERS[p][0]
        rows = slot_of(axis, SIZE[axis] - by, SUM1[p])
        copy = remote(gather1[p].at[rows], other1[p].at[rows], last_send.at[p, by], last_recv.at[p, by], sibling)
        copy.start()
        crossings[p].append(copy)

    sent()

    for p in READY:
        axis1 = ORDERS[p][0]
        for copy in arrivals[p]:
            copy.wait_recv()
        mine = slot(axis1, SUM1[p])
        gather1[p][mine, :] = gather2[p][:SUM1[p], :]
        arrivals[p] = start_all(4, p, axis1, lambda by: gather1[p].at[mine], lambda by: gather1[p].at[mine])

    sent()

    for p in READY:
        across(p, 0)
    for p in READY:
        axis1 = ORDERS[p][0]
        for by, copy in zip(far_last(SIZE[axis1]), reversed(arrivals[p])):
            copy.wait_recv()
            across(p, by)
    for p in READY:
        for j in range(COLS):
            rows = pl.ds(pl.multiple_of(core * HALF + FIRST[p], TILE), PART[p])
            pgrad_ref[rows, j * LANES:(j + 1) * LANES] = gather1[p][j * PART[p]:(j + 1) * PART[p], :]
    for p in READY:
        for copy in crossings[p]:
            copy.wait_recv()
        for j in range(COLS):
            rows = pl.ds(pl.multiple_of((1 - core) * HALF + FIRST[p], TILE), PART[p])
            pgrad_ref[rows, j * LANES:(j + 1) * LANES] = other1[p][j * PART[p]:(j + 1) * PART[p], :]
        started.extend(crossings[p])

    sent()
    sent()


def hand_over(cgrad_ref, pgrad_ref, cgrad_out, pgrad_out, sem):
    copies = []
    for source, target in ((cgrad_ref, cgrad_out), (pgrad_ref, pgrad_out)):
        rows = source.shape[0] // PIECES
        for k in range(PIECES):
            piece = pl.ds(k * rows, rows)
            copies.append(pltpu.make_async_copy(source.at[piece], target.at[piece], sem.at[len(copies)]))
    for copy in copies:
        copy.start()
    for copy in copies:
        copy.wait()


def local(video_emb, captions, projection, labels, log_scale, bias):
    dma = pltpu.SemaphoreType.DMA
    vmem = pltpu.VMEM

    def each(shape_of, dtype=BF16):
        return [vmem(shape_of(p), dtype) for p in range(PARTS)]

    held = [pltpu.with_memory_space_constraint(x, pltpu.HBM) for x in (video_emb, captions, projection, labels)]
    cgrad, pgrad = pl.pallas_call(
        kernel,
        out_shape=(
            jax.ShapeDtypeStruct((ROWS, D), BF16),
            jax.ShapeDtypeStruct((D, E), BF16),
        ),
        in_specs=[pl.BlockSpec(memory_space=pl.ANY)] * 4
        + [pl.BlockSpec(memory_space=pltpu.SMEM)] * 2,
        out_specs=[pl.BlockSpec(memory_space=pltpu.VMEM)] * 2,
        scratch_shapes=[
            vmem((ROWS, E), BF16),
            vmem((ROWS, D), BF16),
            vmem((D, E), BF16),
            vmem((D, ROWS), BF16),
            vmem((ROWS,), jnp.int32),
            vmem((ROWS, E), F32),
            vmem((ROWS, E), BF16),
            vmem((ROWS, 1), F32),
            vmem((ROWS, E), F32),
            vmem((ROWS, E), BF16),
            vmem((ROWS, E), BF16),
            vmem((ROWS, E), BF16),
            vmem((CHUNKS, len(WAYS), CHUNK, E), BF16),
            vmem((CHUNKS, len(WAYS) * CHUNK, E), BF16),
            each(lambda p: (FLAT[p], LANES)),
            each(lambda p: (FLAT[p], LANES)),
            each(lambda p: (FLAT[p], LANES), F32),
            each(lambda p: (FULL1[p], LANES)),
            each(lambda p: (SIZE[ORDERS[p][0]], SUM1[p], LANES)),
            each(lambda p: (FULL2[p], LANES)),
            each(lambda p: (SIZE[ORDERS[p][1]], SUM2[p], LANES)),
            each(lambda p: (SIZE[ORDERS[p][2]], SUM2[p], LANES)),
            each(lambda p: (FULL2[p], LANES)),
            each(lambda p: (FULL1[p], LANES)),
            each(lambda p: (FULL1[p], LANES)),
            dma((4,)),
            dma((CHUNKS, len(WAYS), 2)),
            dma((CHUNKS, len(WAYS), 2)),
            dma((2,)),
            dma((2,)),
            dma((PARTS,)),
            dma((PARTS,)),
            dma((5, PARTS, 8)),
            dma((5, PARTS, 8)),
            dma((PARTS, 8)),
            dma((PARTS, 8)),
            pltpu.SemaphoreType.REGULAR,
        ],
        compiler_params=pltpu.CompilerParams(
            collective_id=0, has_side_effects=True, vmem_limit_bytes=40 << 20
        ),
    )(*held, log_scale, bias)
    return pl.pallas_call(
        hand_over,
        out_shape=(
            jax.ShapeDtypeStruct((ROWS, D), BF16),
            jax.ShapeDtypeStruct((D, E), BF16),
        ),
        in_specs=[pl.BlockSpec(memory_space=pl.ANY)] * 2,
        out_specs=[pl.BlockSpec(memory_space=pl.ANY)] * 2,
        scratch_shapes=[dma((2 * PIECES,))],
        compiler_params=pltpu.CompilerParams(vmem_limit_bytes=1 << 20),
    )(cgrad, pgrad)


def solution(mesh):
    return jax.shard_map(
        local,
        mesh=mesh,
        in_specs=(P("dp", None), P("dp", None), P(), P("dp"), P(), P()),
        out_specs=(P("dp", None), P()),
        check_vma=False,
    )
```

```python
import functools

import jax
import jax.numpy as jnp
from jax import lax
from jax.experimental import pallas as pl
from jax.experimental.pallas import tpu as pltpu
from jax.sharding import PartitionSpec as P

MESH = pl.DeviceIdType.MESH
F32 = jnp.float32
BF16 = jnp.bfloat16

AXES = {"core": (1, 2), "x": (2, 4), "z": (8, 8), "y": (64, 8)}
SIZE = {axis: size for axis, (_, size) in AXES.items()}

ROWS = 384
E = 640
D = 1152
HALF = D // 2
CHUNKS = 3
CHUNK = ROWS // (2 * CHUNKS)
NEAR, REST = 1, 3
WAYS = (("y", 1), ("y", -1), ("z", 1), ("z", -1))
LANES = 128
COLS = E // LANES
TILE = 16

ORDERS = (("x", "y", "z"), ("y", "x", "z"), ("z", "x", "y"))
PART = (224, 176, 176)
FIRST = (0, 224, 400)
PARTS = len(ORDERS)
READY = (1, 2, 0)
PIECES = 3


def up(value, multiple):
    return -(-value // multiple) * multiple


FLAT = tuple(rows * COLS for rows in PART)
SUM1 = tuple(up(-(-FLAT[p] // SIZE[ORDERS[p][0]]), TILE) for p in range(PARTS))
SUM2 = tuple(up(-(-SUM1[p] // SIZE[ORDERS[p][1]]), TILE) for p in range(PARTS))
FULL1 = tuple(SUM1[p] * SIZE[ORDERS[p][0]] for p in range(PARTS))
FULL2 = tuple(SUM2[p] * SIZE[ORDERS[p][1]] for p in range(PARTS))


def place(me, axis):
    stride, size = AXES[axis]
    return lax.rem(lax.div(me, stride), size)


def shifted(me, axis, by):
    stride, size = AXES[axis]
    here = place(me, axis)
    return me + (lax.rem(here + (by + size), size) - here) * stride


def remote(src, dst, send, recv, device):
    return pltpu.make_async_remote_copy(
        src_ref=src, dst_ref=dst, send_sem=send, recv_sem=recv, device_id=(device,), device_id_type=MESH
    )


def far_first(size):
    return sorted(range(1, size), key=lambda by: -min(by, size - by))


def far_last(size):
    return far_first(size)[::-1]


def kernel(
    video_ref, captions_ref, projection_ref, labels_ref, log_scale_ref, bias_ref,
    cgrad_ref, pgrad_ref,
    video, captions, projection, flipped, labels, zf, zc, inv, dz, dh,
    own_core, own_x, relay, pool,
    out_core, in_core, own_term, s1_out, s1_in, s2_out, s2_in, s3_in, gather2, gather1, other1,
    load_sem, hop_send, hop_recv, swap_send, swap_recv, core_send, core_recv,
    stage_send, stage_recv, last_send, last_recv, round_sem, second_sem,
):
    me = lax.axis_index("dp")
    core = place(me, "core")
    sibling = shifted(me, "core", 1)

    barrier = pltpu.get_barrier_semaphore()
    greeted = [*WAYS, ("x", 1), ("x", -1), ("core", 1)]
    for axis, by in greeted:
        pl.semaphore_signal(barrier, inc=1, device_id=(shifted(me, axis, by),), device_id_type=MESH)
    loads = [
        pltpu.make_async_copy(video_ref, video, load_sem.at[0]),
        pltpu.make_async_copy(captions_ref, captions, load_sem.at[1]),
        pltpu.make_async_copy(projection_ref, projection, load_sem.at[2]),
        pltpu.make_async_copy(labels_ref, labels, load_sem.at[3]),
    ]
    for load in loads:
        load.start()
    pl.semaphore_wait(barrier, len(greeted))
    first_round = [*WAYS, ("x", 1), ("x", -1)]
    for axis, by in first_round:
        pl.semaphore_signal(round_sem, inc=1, device_id=(shifted(me, axis, by),), device_id_type=MESH)
    loads[0].wait()

    hops = []
    for q in range(CHUNKS):
        for w, (axis, way) in enumerate(WAYS):
            rows = pl.ds(((0 if way > 0 else CHUNKS) + q) * CHUNK, CHUNK)
            first = remote(
                video.at[rows], relay.at[q, w], hop_send.at[q, w, 0], hop_recv.at[q, w, 0], shifted(me, axis, way * NEAR)
            )
            second = remote(
                relay.at[q, w], pool.at[q, pl.ds(w * CHUNK, CHUNK)], hop_send.at[q, w, 1], hop_recv.at[q, w, 1],
                shifted(me, axis, way * REST),
            )
            first.start()
            hops.append((first, second))
    swap_core = remote(video, own_core, swap_send.at[1], swap_recv.at[1], sibling)
    swap_core.start()

    def pass_on(q):
        for first, second in hops[q * len(WAYS):(q + 1) * len(WAYS)]:
            first.wait_recv()
            second.start()

    pl.semaphore_wait(round_sem, len(first_round))
    for axis, way in WAYS:
        pl.semaphore_signal(second_sem, inc=1, device_id=(shifted(me, axis, 2 * way),), device_id_type=MESH)
    swap_x = remote(video, own_x, swap_send.at[0], swap_recv.at[0], shifted(me, "x", 2))
    swap_x.start()

    scale = jnp.exp(jnp.full((1, 1), log_scale_ref[0], F32))
    shift = bias_ref[0]

    loads[1].wait()
    loads[2].wait()
    loads[3].wait()
    hidden = jnp.dot(captions[...], projection[...], preferred_element_type=F32)
    inverse = lax.rsqrt(jnp.sum(hidden * hidden, axis=-1, keepdims=True) + 1e-06)
    unit = hidden * inverse
    zf[...] = unit
    zc[...] = unit.astype(BF16)
    inv[...] = inverse

    def pairing(rows, sign=None):
        raw = rows.astype(F32)
        zv = (raw * lax.rsqrt(jnp.sum(raw * raw, axis=-1, keepdims=True) + 1e-06)).astype(BF16)
        logits = scale * lax.dot_general(
            zc[...], zv, (((1,), (1,)), ((), ())), preferred_element_type=F32
        ) + shift
        if sign is None:
            weight = 1.0 / (1.0 + jnp.exp(-logits))
        else:
            weight = sign / (1.0 + jnp.exp(-sign * logits))
        return jnp.dot(weight.astype(BF16), zv, preferred_element_type=F32)

    pl.semaphore_wait(second_sem, len(WAYS))
    pass_on(0)
    row = lax.broadcasted_iota(jnp.int32, (ROWS, ROWS), 0)
    column = lax.broadcasted_iota(jnp.int32, (ROWS, ROWS), 1)
    sign = jnp.where((row == column) & (labels[...].reshape(1, ROWS) == 1), -1.0, 1.0).astype(F32)
    dz[...] = pairing(video[...], sign)
    for q in range(1, CHUNKS):
        pass_on(q)
    flipped[...] = captions[...].T
    swap_core.wait_recv()
    dz[...] += pairing(own_core[...])
    swap_x.wait_recv()
    dz[...] += pairing(own_x[...])
    for q in range(CHUNKS):
        for _, second in hops[q * len(WAYS):(q + 1) * len(WAYS)]:
            second.wait_recv()
        if q < CHUNKS - 1:
            dz[...] += pairing(pool[q])

    total = scale * (dz[...] + pairing(pool[CHUNKS - 1]))
    along = jnp.sum(zf[...] * total, axis=-1, keepdims=True)
    dh[...] = (inv[...] * (total - zf[...] * along)).astype(BF16)

    def term(half, part):
        rows = pl.ds(pl.multiple_of(half * HALF + FIRST[part], TILE), PART[part])
        return jnp.dot(flipped[rows, :], dh[...], preferred_element_type=F32)

    to_core = []
    for p in range(PARTS):
        value = term(1 - core, p).astype(BF16)
        for j in range(COLS):
            out_core[p][j * PART[p]:(j + 1) * PART[p], :] = value[:, j * LANES:(j + 1) * LANES]
        copy = remote(out_core[p], in_core[p], core_send.at[p], core_recv.at[p], sibling)
        copy.start()
        to_core.append(copy)
    for p in range(PARTS):
        value = term(core, p)
        for j in range(COLS):
            own_term[p][j * PART[p]:(j + 1) * PART[p], :] = value[:, j * LANES:(j + 1) * LANES]

    pending = [copy for pair in hops for copy in pair] + [swap_x, swap_core, *to_core]

    def sent():
        for copy in pending:
            copy.wait_send()
        pending[:] = started
        started.clear()

    started = []

    def start_all(stage, p, axis, src_of, dst_of):
        copies = []
        for by in far_first(SIZE[axis]):
            copy = remote(
                src_of(by), dst_of(by), stage_send.at[stage, p, by], stage_recv.at[stage, p, by], shifted(me, axis, by)
            )
            copy.start()
            copies.append(copy)
        started.extend(copies)
        return copies

    def slot(axis, rows):
        return pl.ds(pl.multiple_of(place(me, axis) * rows, TILE), rows)

    def slot_of(axis, by, rows):
        return pl.ds(pl.multiple_of(lax.rem(place(me, axis) + by, SIZE[axis]) * rows, TILE), rows)

    arrivals = [None] * PARTS
    for p, (axis, _, _) in enumerate(ORDERS):
        to_core[p].wait_recv()
        s1_out[p][:FLAT[p], :] = (own_term[p][...] + in_core[p][...].astype(F32)).astype(BF16)
        if FULL1[p] > FLAT[p]:
            s1_out[p][FLAT[p]:, :] = jnp.zeros((FULL1[p] - FLAT[p], LANES), BF16)
        arrivals[p] = start_all(
            0, p, axis, lambda by: s1_out[p].at[slot_of(axis, by, SUM1[p])], lambda by: s1_in[p].at[by]
        )

    cgrad_ref[...] = lax.dot_general(
        dh[...], projection[...], (((1,), (1,)), ((), ())), preferred_element_type=F32
    ).astype(BF16)

    sent()

    for p, (axis1, axis2, _) in enumerate(ORDERS):
        for copy in arrivals[p]:
            copy.wait_recv()
        value = s1_out[p][slot(axis1, SUM1[p]), :].astype(F32)
        for by in range(1, SIZE[axis1]):
            value += s1_in[p][by].astype(F32)
        s2_out[p][:SUM1[p], :] = value.astype(BF16)
        if FULL2[p] > SUM1[p]:
            s2_out[p][SUM1[p]:, :] = jnp.zeros((FULL2[p] - SUM1[p], LANES), BF16)
        arrivals[p] = start_all(
            1, p, axis2, lambda by: s2_out[p].at[slot_of(axis2, by, SUM2[p])], lambda by: s2_in[p].at[by]
        )

    sent()

    for p, (_, axis2, axis3) in enumerate(ORDERS):
        for copy in arrivals[p]:
            copy.wait_recv()
        value = s2_out[p][slot(axis2, SUM2[p]), :].astype(F32)
        for by in range(1, SIZE[axis2]):
            value += s2_in[p][by].astype(F32)
        here = place(me, axis3)
        s3_in[p][here] = value.astype(BF16)
        arrivals[p] = start_all(2, p, axis3, lambda by: s3_in[p].at[here], lambda by: s3_in[p].at[here])

    devices = 1
    for size in SIZE.values():
        devices *= size

    sent()

    for p, (_, axis2, axis3) in enumerate(ORDERS):
        for copy in arrivals[p]:
            copy.wait_recv()
        value = s3_in[p][0].astype(F32)
        for k in range(1, SIZE[axis3]):
            value += s3_in[p][k].astype(F32)
        mine = slot(axis2, SUM2[p])
        gather2[p][mine, :] = (value / devices).astype(BF16)
        arrivals[p] = start_all(3, p, axis2, lambda by: gather2[p].at[mine], lambda by: gather2[p].at[mine])

    crossings = [[] for _ in range(PARTS)]

    def across(p, by):
        axis = ORDERS[p][0]
        rows = slot_of(axis, SIZE[axis] - by, SUM1[p])
        copy = remote(gather1[p].at[rows], other1[p].at[rows], last_send.at[p, by], last_recv.at[p, by], sibling)
        copy.start()
        crossings[p].append(copy)

    sent()

    for p in READY:
        axis1 = ORDERS[p][0]
        for copy in arrivals[p]:
            copy.wait_recv()
        mine = slot(axis1, SUM1[p])
        gather1[p][mine, :] = gather2[p][:SUM1[p], :]
        arrivals[p] = start_all(4, p, axis1, lambda by: gather1[p].at[mine], lambda by: gather1[p].at[mine])

    sent()

    for p in READY:
        across(p, 0)
    for p in READY:
        axis1 = ORDERS[p][0]
        for by, copy in zip(far_last(SIZE[axis1]), reversed(arrivals[p])):
            copy.wait_recv()
            across(p, by)
    for p in READY:
        for j in range(COLS):
            rows = pl.ds(pl.multiple_of(core * HALF + FIRST[p], TILE), PART[p])
            pgrad_ref[rows, j * LANES:(j + 1) * LANES] = gather1[p][j * PART[p]:(j + 1) * PART[p], :]
    for p in READY:
        for copy in crossings[p]:
            copy.wait_recv()
        for j in range(COLS):
            rows = pl.ds(pl.multiple_of((1 - core) * HALF + FIRST[p], TILE), PART[p])
            pgrad_ref[rows, j * LANES:(j + 1) * LANES] = other1[p][j * PART[p]:(j + 1) * PART[p], :]
        started.extend(crossings[p])

    sent()
    sent()


def hand_over(cgrad_ref, pgrad_ref, cgrad_out, pgrad_out, sem):
    copies = []
    for source, target in ((cgrad_ref, cgrad_out), (pgrad_ref, pgrad_out)):
        rows = source.shape[0] // PIECES
        for k in range(PIECES):
            piece = pl.ds(k * rows, rows)
            copies.append(pltpu.make_async_copy(source.at[piece], target.at[piece], sem.at[len(copies)]))
    for copy in copies:
        copy.start()
    for copy in copies:
        copy.wait()


def local(video_emb, captions, projection, labels, log_scale, bias):
    dma = pltpu.SemaphoreType.DMA
    vmem = pltpu.VMEM

    def each(shape_of, dtype=BF16):
        return [vmem(shape_of(p), dtype) for p in range(PARTS)]

    held = [pltpu.with_memory_space_constraint(x, pltpu.HBM) for x in (video_emb, captions, projection, labels)]
    cgrad, pgrad = pl.pallas_call(
        kernel,
        out_shape=(
            jax.ShapeDtypeStruct((ROWS, D), BF16),
            jax.ShapeDtypeStruct((D, E), BF16),
        ),
        in_specs=[pl.BlockSpec(memory_space=pl.ANY)] * 4
        + [pl.BlockSpec(memory_space=pltpu.SMEM)] * 2,
        out_specs=[pl.BlockSpec(memory_space=pltpu.VMEM)] * 2,
        scratch_shapes=[
            vmem((ROWS, E), BF16),
            vmem((ROWS, D), BF16),
            vmem((D, E), BF16),
            vmem((D, ROWS), BF16),
            vmem((ROWS,), jnp.int32),
            vmem((ROWS, E), F32),
            vmem((ROWS, E), BF16),
            vmem((ROWS, 1), F32),
            vmem((ROWS, E), F32),
            vmem((ROWS, E), BF16),
            vmem((ROWS, E), BF16),
            vmem((ROWS, E), BF16),
            vmem((CHUNKS, len(WAYS), CHUNK, E), BF16),
            vmem((CHUNKS, len(WAYS) * CHUNK, E), BF16),
            each(lambda p: (FLAT[p], LANES)),
            each(lambda p: (FLAT[p], LANES)),
            each(lambda p: (FLAT[p], LANES), F32),
            each(lambda p: (FULL1[p], LANES)),
            each(lambda p: (SIZE[ORDERS[p][0]], SUM1[p], LANES)),
            each(lambda p: (FULL2[p], LANES)),
            each(lambda p: (SIZE[ORDERS[p][1]], SUM2[p], LANES)),
            each(lambda p: (SIZE[ORDERS[p][2]], SUM2[p], LANES)),
            each(lambda p: (FULL2[p], LANES)),
            each(lambda p: (FULL1[p], LANES)),
            each(lambda p: (FULL1[p], LANES)),
            dma((4,)),
            dma((CHUNKS, len(WAYS), 2)),
            dma((CHUNKS, len(WAYS), 2)),
            dma((2,)),
            dma((2,)),
            dma((PARTS,)),
            dma((PARTS,)),
            dma((5, PARTS, 8)),
            dma((5, PARTS, 8)),
            dma((PARTS, 8)),
            dma((PARTS, 8)),
            pltpu.SemaphoreType.REGULAR,
            pltpu.SemaphoreType.REGULAR,
        ],
        compiler_params=pltpu.CompilerParams(
            collective_id=0, has_side_effects=True, vmem_limit_bytes=40 << 20
        ),
    )(*held, log_scale, bias)
    return pl.pallas_call(
        hand_over,
        out_shape=(
            jax.ShapeDtypeStruct((ROWS, D), BF16),
            jax.ShapeDtypeStruct((D, E), BF16),
        ),
        in_specs=[pl.BlockSpec(memory_space=pl.ANY)] * 2,
        out_specs=[pl.BlockSpec(memory_space=pl.ANY)] * 2,
        scratch_shapes=[dma((2 * PIECES,))],
        compiler_params=pltpu.CompilerParams(vmem_limit_bytes=1 << 20),
    )(cgrad, pgrad)


def solution(mesh):
    return jax.shard_map(
        local,
        mesh=mesh,
        in_specs=(P("dp", None), P("dp", None), P(), P("dp"), P(), P()),
        out_specs=(P("dp", None), P()),
        check_vma=False,
    )
```

```python
import functools

import jax
import jax.numpy as jnp
from jax import lax
from jax.experimental import pallas as pl
from jax.experimental.pallas import tpu as pltpu
from jax.sharding import PartitionSpec as P

MESH = pl.DeviceIdType.MESH
F32 = jnp.float32
BF16 = jnp.bfloat16

AXES = {"core": (1, 2), "x": (2, 4), "z": (8, 8), "y": (64, 8)}
SIZE = {axis: size for axis, (_, size) in AXES.items()}

ROWS = 384
E = 640
D = 1152
HALF = D // 2
CHUNKS = 2
CHUNK = ROWS // (2 * CHUNKS)
NEAR, REST = 1, 3
WAYS = (("y", 1), ("y", -1), ("z", 1), ("z", -1))
LANES = 128
COLS = E // LANES
TILE = 16

ORDERS = (("x", "y", "z"), ("y", "x", "z"), ("z", "x", "y"))
PART = (224, 176, 176)
FIRST = (0, 224, 400)
PARTS = len(ORDERS)
READY = (1, 2, 0)
PIECES = 3


def up(value, multiple):
    return -(-value // multiple) * multiple


FLAT = tuple(rows * COLS for rows in PART)
SUM1 = tuple(up(-(-FLAT[p] // SIZE[ORDERS[p][0]]), TILE) for p in range(PARTS))
SUM2 = tuple(up(-(-SUM1[p] // SIZE[ORDERS[p][1]]), TILE) for p in range(PARTS))
FULL1 = tuple(SUM1[p] * SIZE[ORDERS[p][0]] for p in range(PARTS))
FULL2 = tuple(SUM2[p] * SIZE[ORDERS[p][1]] for p in range(PARTS))


def place(me, axis):
    stride, size = AXES[axis]
    return lax.rem(lax.div(me, stride), size)


def shifted(me, axis, by):
    stride, size = AXES[axis]
    here = place(me, axis)
    return me + (lax.rem(here + (by + size), size) - here) * stride


def remote(src, dst, send, recv, device):
    return pltpu.make_async_remote_copy(
        src_ref=src, dst_ref=dst, send_sem=send, recv_sem=recv, device_id=(device,), device_id_type=MESH
    )


def far_first(size):
    return sorted(range(1, size), key=lambda by: -min(by, size - by))


def far_last(size):
    return far_first(size)[::-1]


def kernel(
    video_ref, captions_ref, projection_ref, labels_ref, log_scale_ref, bias_ref,
    cgrad_ref, pgrad_ref,
    video, captions, projection, flipped, labels, zf, zc, inv, dz, dh,
    own_core, own_x, relay, pool,
    out_core, in_core, own_term, s1_out, s1_in, s2_out, s2_in, s3_in, gather2, gather1, other1,
    load_sem, hop_send, hop_recv, swap_send, swap_recv, core_send, core_recv,
    stage_send, stage_recv, last_send, last_recv, round_sem, second_sem,
):
    me = lax.axis_index("dp")
    core = place(me, "core")
    sibling = shifted(me, "core", 1)

    barrier = pltpu.get_barrier_semaphore()
    greeted = [*WAYS, ("x", 1), ("x", -1), ("core", 1)]
    for axis, by in greeted:
        pl.semaphore_signal(barrier, inc=1, device_id=(shifted(me, axis, by),), device_id_type=MESH)
    loads = [
        pltpu.make_async_copy(video_ref, video, load_sem.at[0]),
        pltpu.make_async_copy(captions_ref, captions, load_sem.at[1]),
        pltpu.make_async_copy(projection_ref, projection, load_sem.at[2]),
        pltpu.make_async_copy(labels_ref, labels, load_sem.at[3]),
    ]
    for load in loads:
        load.start()
    pl.semaphore_wait(barrier, len(greeted))
    first_round = [*WAYS, ("x", 1), ("x", -1)]
    for axis, by in first_round:
        pl.semaphore_signal(round_sem, inc=1, device_id=(shifted(me, axis, by),), device_id_type=MESH)
    loads[0].wait()

    hops = []
    for q in range(CHUNKS):
        for w, (axis, way) in enumerate(WAYS):
            rows = pl.ds(((0 if way > 0 else CHUNKS) + q) * CHUNK, CHUNK)
            first = remote(
                video.at[rows], relay.at[q, w], hop_send.at[q, w, 0], hop_recv.at[q, w, 0], shifted(me, axis, way * NEAR)
            )
            second = remote(
                relay.at[q, w], pool.at[q, pl.ds(w * CHUNK, CHUNK)], hop_send.at[q, w, 1], hop_recv.at[q, w, 1],
                shifted(me, axis, way * REST),
            )
            first.start()
            hops.append((first, second))
    swap_core = remote(video, own_core, swap_send.at[1], swap_recv.at[1], sibling)
    swap_core.start()

    def pass_on(q):
        for first, second in hops[q * len(WAYS):(q + 1) * len(WAYS)]:
            first.wait_recv()
            second.start()

    pl.semaphore_wait(round_sem, len(first_round))
    for axis, way in WAYS:
        pl.semaphore_signal(second_sem, inc=1, device_id=(shifted(me, axis, 2 * way),), device_id_type=MESH)
    swap_x = remote(video, own_x, swap_send.at[0], swap_recv.at[0], shifted(me, "x", 2))
    swap_x.start()

    scale = jnp.exp(jnp.full((1, 1), log_scale_ref[0], F32))
    shift = bias_ref[0]

    loads[1].wait()
    loads[2].wait()
    loads[3].wait()
    hidden = jnp.dot(captions[...], projection[...], preferred_element_type=F32)
    inverse = lax.rsqrt(jnp.sum(hidden * hidden, axis=-1, keepdims=True) + 1e-06)
    unit = hidden * inverse
    zf[...] = unit
    zc[...] = unit.astype(BF16)
    inv[...] = inverse

    def pairing(rows, sign=None):
        raw = rows.astype(F32)
        zv = (raw * lax.rsqrt(jnp.sum(raw * raw, axis=-1, keepdims=True) + 1e-06)).astype(BF16)
        logits = scale * lax.dot_general(
            zc[...], zv, (((1,), (1,)), ((), ())), preferred_element_type=F32
        ) + shift
        if sign is None:
            weight = 1.0 / (1.0 + jnp.exp(-logits))
        else:
            weight = sign / (1.0 + jnp.exp(-sign * logits))
        return jnp.dot(weight.astype(BF16), zv, preferred_element_type=F32)

    pl.semaphore_wait(second_sem, len(WAYS))
    pass_on(0)
    row = lax.broadcasted_iota(jnp.int32, (ROWS, ROWS), 0)
    column = lax.broadcasted_iota(jnp.int32, (ROWS, ROWS), 1)
    sign = jnp.where((row == column) & (labels[...].reshape(1, ROWS) == 1), -1.0, 1.0).astype(F32)
    dz[...] = pairing(video[...], sign)
    for q in range(1, CHUNKS):
        pass_on(q)
    flipped[...] = captions[...].T
    swap_core.wait_recv()
    dz[...] += pairing(own_core[...])
    swap_x.wait_recv()
    dz[...] += pairing(own_x[...])
    for q in range(CHUNKS):
        for _, second in hops[q * len(WAYS):(q + 1) * len(WAYS)]:
            second.wait_recv()
        if q < CHUNKS - 1:
            dz[...] += pairing(pool[q])

    total = scale * (dz[...] + pairing(pool[CHUNKS - 1]))
    along = jnp.sum(zf[...] * total, axis=-1, keepdims=True)
    dh[...] = (inv[...] * (total - zf[...] * along)).astype(BF16)

    def term(half, part):
        rows = pl.ds(pl.multiple_of(half * HALF + FIRST[part], TILE), PART[part])
        return jnp.dot(flipped[rows, :], dh[...], preferred_element_type=F32)

    to_core = []
    for p in range(PARTS):
        value = term(1 - core, p).astype(BF16)
        for j in range(COLS):
            out_core[p][j * PART[p]:(j + 1) * PART[p], :] = value[:, j * LANES:(j + 1) * LANES]
        copy = remote(out_core[p], in_core[p], core_send.at[p], core_recv.at[p], sibling)
        copy.start()
        to_core.append(copy)
    for p in range(PARTS):
        value = term(core, p)
        for j in range(COLS):
            own_term[p][j * PART[p]:(j + 1) * PART[p], :] = value[:, j * LANES:(j + 1) * LANES]

    pending = [copy for pair in hops for copy in pair] + [swap_x, swap_core, *to_core]

    def sent():
        for copy in pending:
            copy.wait_send()
        pending[:] = started
        started.clear()

    started = []

    def start_all(stage, p, axis, src_of, dst_of):
        copies = []
        for by in far_first(SIZE[axis]):
            copy = remote(
                src_of(by), dst_of(by), stage_send.at[stage, p, by], stage_recv.at[stage, p, by], shifted(me, axis, by)
            )
            copy.start()
            copies.append(copy)
        started.extend(copies)
        return copies

    def slot(axis, rows):
        return pl.ds(pl.multiple_of(place(me, axis) * rows, TILE), rows)

    def slot_of(axis, by, rows):
        return pl.ds(pl.multiple_of(lax.rem(place(me, axis) + by, SIZE[axis]) * rows, TILE), rows)

    arrivals = [None] * PARTS
    for p, (axis, _, _) in enumerate(ORDERS):
        to_core[p].wait_recv()
        s1_out[p][:FLAT[p], :] = (own_term[p][...] + in_core[p][...].astype(F32)).astype(BF16)
        if FULL1[p] > FLAT[p]:
            s1_out[p][FLAT[p]:, :] = jnp.zeros((FULL1[p] - FLAT[p], LANES), BF16)
        arrivals[p] = start_all(
            0, p, axis, lambda by: s1_out[p].at[slot_of(axis, by, SUM1[p])], lambda by: s1_in[p].at[by]
        )

    cgrad_ref[...] = lax.dot_general(
        dh[...], projection[...], (((1,), (1,)), ((), ())), preferred_element_type=F32
    ).astype(BF16)

    sent()

    for p, (axis1, axis2, _) in enumerate(ORDERS):
        for copy in arrivals[p]:
            copy.wait_recv()
        value = s1_out[p][slot(axis1, SUM1[p]), :].astype(F32)
        for by in range(1, SIZE[axis1]):
            value += s1_in[p][by].astype(F32)
        s2_out[p][:SUM1[p], :] = value.astype(BF16)
        if FULL2[p] > SUM1[p]:
            s2_out[p][SUM1[p]:, :] = jnp.zeros((FULL2[p] - SUM1[p], LANES), BF16)
        arrivals[p] = start_all(
            1, p, axis2, lambda by: s2_out[p].at[slot_of(axis2, by, SUM2[p])], lambda by: s2_in[p].at[by]
        )

    sent()

    for p, (_, axis2, axis3) in enumerate(ORDERS):
        for copy in arrivals[p]:
            copy.wait_recv()
        value = s2_out[p][slot(axis2, SUM2[p]), :].astype(F32)
        for by in range(1, SIZE[axis2]):
            value += s2_in[p][by].astype(F32)
        here = place(me, axis3)
        s3_in[p][here] = value.astype(BF16)
        arrivals[p] = start_all(2, p, axis3, lambda by: s3_in[p].at[here], lambda by: s3_in[p].at[here])

    devices = 1
    for size in SIZE.values():
        devices *= size

    sent()

    for p, (_, axis2, axis3) in enumerate(ORDERS):
        for copy in arrivals[p]:
            copy.wait_recv()
        value = s3_in[p][0].astype(F32)
        for k in range(1, SIZE[axis3]):
            value += s3_in[p][k].astype(F32)
        mine = slot(axis2, SUM2[p])
        gather2[p][mine, :] = (value / devices).astype(BF16)
        arrivals[p] = start_all(3, p, axis2, lambda by: gather2[p].at[mine], lambda by: gather2[p].at[mine])

    crossings = [[] for _ in range(PARTS)]

    def across(p, by):
        axis = ORDERS[p][0]
        rows = slot_of(axis, SIZE[axis] - by, SUM1[p])
        copy = remote(gather1[p].at[rows], other1[p].at[rows], last_send.at[p, by], last_recv.at[p, by], sibling)
        copy.start()
        crossings[p].append(copy)

    sent()

    for p in READY:
        axis1 = ORDERS[p][0]
        for copy in arrivals[p]:
            copy.wait_recv()
        mine = slot(axis1, SUM1[p])
        gather1[p][mine, :] = gather2[p][:SUM1[p], :]
        arrivals[p] = start_all(4, p, axis1, lambda by: gather1[p].at[mine], lambda by: gather1[p].at[mine])

    sent()

    for p in READY:
        across(p, 0)
    for p in READY:
        axis1 = ORDERS[p][0]
        for by, copy in zip(far_last(SIZE[axis1]), reversed(arrivals[p])):
            copy.wait_recv()
            across(p, by)
    for p in READY:
        for j in range(COLS):
            rows = pl.ds(pl.multiple_of(core * HALF + FIRST[p], TILE), PART[p])
            pgrad_ref[rows, j * LANES:(j + 1) * LANES] = gather1[p][j * PART[p]:(j + 1) * PART[p], :]
    for p in READY:
        for copy in crossings[p]:
            copy.wait_recv()
        for j in range(COLS):
            rows = pl.ds(pl.multiple_of((1 - core) * HALF + FIRST[p], TILE), PART[p])
            pgrad_ref[rows, j * LANES:(j + 1) * LANES] = other1[p][j * PART[p]:(j + 1) * PART[p], :]
        started.extend(crossings[p])

    sent()
    sent()


def hand_over(cgrad_ref, pgrad_ref, cgrad_out, pgrad_out, sem):
    copies = []
    for source, target in ((cgrad_ref, cgrad_out), (pgrad_ref, pgrad_out)):
        rows = source.shape[0] // PIECES
        for k in range(PIECES):
            piece = pl.ds(k * rows, rows)
            copies.append(pltpu.make_async_copy(source.at[piece], target.at[piece], sem.at[len(copies)]))
    for copy in copies:
        copy.start()
    for copy in copies:
        copy.wait()


def local(video_emb, captions, projection, labels, log_scale, bias):
    dma = pltpu.SemaphoreType.DMA
    vmem = pltpu.VMEM

    def each(shape_of, dtype=BF16):
        return [vmem(shape_of(p), dtype) for p in range(PARTS)]

    held = [pltpu.with_memory_space_constraint(x, pltpu.HBM) for x in (video_emb, captions, projection, labels)]
    cgrad, pgrad = pl.pallas_call(
        kernel,
        out_shape=(
            jax.ShapeDtypeStruct((ROWS, D), BF16),
            jax.ShapeDtypeStruct((D, E), BF16),
        ),
        in_specs=[pl.BlockSpec(memory_space=pl.ANY)] * 4
        + [pl.BlockSpec(memory_space=pltpu.SMEM)] * 2,
        out_specs=[pl.BlockSpec(memory_space=pltpu.VMEM)] * 2,
        scratch_shapes=[
            vmem((ROWS, E), BF16),
            vmem((ROWS, D), BF16),
            vmem((D, E), BF16),
            vmem((D, ROWS), BF16),
            vmem((ROWS,), jnp.int32),
            vmem((ROWS, E), F32),
            vmem((ROWS, E), BF16),
            vmem((ROWS, 1), F32),
            vmem((ROWS, E), F32),
            vmem((ROWS, E), BF16),
            vmem((ROWS, E), BF16),
            vmem((ROWS, E), BF16),
            vmem((CHUNKS, len(WAYS), CHUNK, E), BF16),
            vmem((CHUNKS, len(WAYS) * CHUNK, E), BF16),
            each(lambda p: (FLAT[p], LANES)),
            each(lambda p: (FLAT[p], LANES)),
            each(lambda p: (FLAT[p], LANES), F32),
            each(lambda p: (FULL1[p], LANES)),
            each(lambda p: (SIZE[ORDERS[p][0]], SUM1[p], LANES)),
            each(lambda p: (FULL2[p], LANES)),
            each(lambda p: (SIZE[ORDERS[p][1]], SUM2[p], LANES)),
            each(lambda p: (SIZE[ORDERS[p][2]], SUM2[p], LANES)),
            each(lambda p: (FULL2[p], LANES)),
            each(lambda p: (FULL1[p], LANES)),
            each(lambda p: (FULL1[p], LANES)),
            dma((4,)),
            dma((CHUNKS, len(WAYS), 2)),
            dma((CHUNKS, len(WAYS), 2)),
            dma((2,)),
            dma((2,)),
            dma((PARTS,)),
            dma((PARTS,)),
            dma((5, PARTS, 8)),
            dma((5, PARTS, 8)),
            dma((PARTS, 8)),
            dma((PARTS, 8)),
            pltpu.SemaphoreType.REGULAR,
            pltpu.SemaphoreType.REGULAR,
        ],
        compiler_params=pltpu.CompilerParams(
            collective_id=0, has_side_effects=True, vmem_limit_bytes=40 << 20
        ),
    )(*held, log_scale, bias)
    return pl.pallas_call(
        hand_over,
        out_shape=(
            jax.ShapeDtypeStruct((ROWS, D), BF16),
            jax.ShapeDtypeStruct((D, E), BF16),
        ),
        in_specs=[pl.BlockSpec(memory_space=pl.ANY)] * 2,
        out_specs=[pl.BlockSpec(memory_space=pl.ANY)] * 2,
        scratch_shapes=[dma((2 * PIECES,))],
        compiler_params=pltpu.CompilerParams(vmem_limit_bytes=1 << 20),
    )(cgrad, pgrad)


def solution(mesh):
    return jax.shard_map(
        local,
        mesh=mesh,
        in_specs=(P("dp", None), P("dp", None), P(), P("dp"), P(), P()),
        out_specs=(P("dp", None), P()),
        check_vma=False,
    )
```
